32 devices in a mesh: subj: 16 (over z, y, x), vert: 2 (over core).
Axes of the slice: x: 2, y: 2, z: 4, core: 2. Of those that a mesh axis runs over, the one named last changes fastest.
Arguments:
- data: bfloat16 [32, 256, 4096], P('subj', None, 'vert'), may hold values from -6 to 6
- template: bfloat16 [256, 4096], P(None, 'vert'), may hold values from -6 to 6
- centres: int32 [32], P('vert'), may hold values from 0 to 4095, as said below
- neighbours: int32 [32, 128], P('vert'), may hold values from -128 to 127, as said below
Outputs:
- aligned: bfloat16 [32, 256, 4096], P('subj', None, 'vert')
- new_template: float32 [256, 4096], P(None, 'vert')
The draws below stay inside these ranges and needn't reach their ends.
Inputs may be any that keep to these rules, and one draw needn't show every extreme that they name: The 16 centres of each aligned block of 16 entries are distinct vertices of the matching block of 2048 vertices, and include that block's first and last vertex. `neighbours`: A searchlight's 128 offsets are distinct and include -128 and 127.
All inputs are finite; a program needn't handle non-finite values.
Results may differ from the reference program's by a relative error of at most 0.0005.
Values may be sent and summed in bfloat16 or wider, within the bound.
No kernel may reach another device: no remote copies, remote signals or barrier semaphores. Data moves between devices by JAX's collectives and lax.ppermute only.
A program may use at most 64 MiB of HBM per device.

```python
import jax
import jax.numpy as jnp
from jax import lax

K = 128
TF = 256
NS_STEPS = 4
VD = 2048
CEN_DEV = 16
SUBJECTS = 32
VERTS = 4096
CENTRES = 32


def draw_centres(key, part):
    blocks = CENTRES // CEN_DEV
    keys = jax.random.split(key, blocks)

    def one_block(block_key, index):
        inner = jax.random.permutation(block_key, VD - 2)[:CEN_DEV - 2] + 1
        ends = jnp.array([0, VD - 1], jnp.int32)
        return jnp.concatenate([ends, inner.astype(jnp.int32)]) + index * VD
    return jax.vmap(one_block)(keys, jnp.arange(blocks, dtype=jnp.int32)).reshape(-1).astype(jnp.int32)


def draw_neighbours(key, part):
    keys = jax.random.split(jax.random.fold_in(key, 7), CENTRES)

    def one_light(light_key):
        inner = jax.random.permutation(light_key, 2 * K - 2)[:K - 2] + 1 - K
        ends = jnp.array([-K, K - 1], jnp.int32)
        return jnp.concatenate([ends, inner.astype(jnp.int32)])
    return jax.vmap(one_light)(keys).astype(jnp.int32)


def level_of(rng, shape, cuts, smallest, high):
    def one(axis_at, blocks):
        heights = jax.random.uniform(jax.random.fold_in(jax.random.fold_in(rng, 6), axis_at), (blocks,), jnp.float32, smallest / len(cuts), high / len(cuts))
        return jnp.repeat(jnp.exp(heights), shape[axis_at] // blocks).reshape((-1,) + (1,) * (len(shape) - axis_at - 1))

    gain = one(*cuts[0])
    for cut in cuts[1:]:
        gain = gain * one(*cut)
    return gain


def gaussian(stream_key, dims, scale, limit, pieces=(), kind=jnp.bfloat16):
    result = jax.random.normal(stream_key, dims, jnp.float32) * scale
    if len(pieces) > 0:
        result = level_of(stream_key, dims, pieces, -0.22, 0.18) * result
    return jnp.clip(result, min=-limit, max=limit).astype(kind)


def setup_inputs(seed: int = 0) -> dict:
    arg_keys = jax.random.split(jax.random.key(seed), 5)
    data = gaussian(arg_keys[0], (SUBJECTS, TF, VERTS), 1.0, 6.0, ((0, 16), (2, 2)))
    template = gaussian(arg_keys[1], (TF, VERTS), 1.0, 6.0, ((1, 2),))
    centres = draw_centres(jax.random.fold_in(arg_keys[4], 71), 0)
    neighbours = draw_neighbours(jax.random.fold_in(arg_keys[4], 71), 0)
    return dict(data=data, template=template, centres=centres, neighbours=neighbours)


def polar_factor(cross_cov):
    norm_sq = lax.optimization_barrier(jnp.sum(cross_cov * cross_cov, axis=(-2, -1), keepdims=True))
    factor = cross_cov / jnp.sqrt(norm_sq + 1e-06)
    for sweep in range(NS_STEPS):
        gram_mat = jnp.einsum('...kj,...ki->...ji', factor, factor, precision=lax.Precision.HIGHEST)
        factor = 1.5 * factor - 0.5 * jnp.einsum('...kj,...ji->...ki', factor, gram_mat, precision=lax.Precision.HIGHEST)
    return factor

def reference(data, template, centres, neighbours):
    halo_width = neighbours.shape[1]
    n_verts = data.shape[2]
    n_frames = data.shape[1]
    places = centres[:, None] + halo_width + neighbours
    flat_pos = places.reshape(-1).astype(jnp.int32)
    hit_counts = jnp.zeros((n_verts + 2 * halo_width,), jnp.float32).at[flat_pos].add(1.0)
    divisor = jnp.maximum(hit_counts[halo_width:halo_width + n_verts], 1.0)
    padded_template = jnp.pad(template, ((0, 0), (halo_width, halo_width)))
    template_cols = padded_template[:, flat_pos].reshape(n_frames, -1, halo_width).astype(jnp.float32)

    def one_subject(carry, frames):
        padded = jnp.pad(frames, ((0, 0), (halo_width, halo_width)))
        picked = padded[:, flat_pos].reshape(n_frames, -1, halo_width).astype(jnp.float32)
        cross_cov = jnp.einsum('tck,tcj->ckj', picked, template_cols, precision=lax.Precision.HIGHEST)
        rotation = polar_factor(cross_cov)
        rotated = jnp.einsum('tck,ckj->tcj', picked, rotation, precision=lax.Precision.HIGHEST)
        summed = jnp.zeros((n_frames, n_verts + 2 * halo_width), jnp.float32).at[:, flat_pos].add(rotated.reshape(n_frames, -1))
        mapped = summed[:, halo_width:halo_width + n_verts] / divisor
        return (carry + mapped, mapped.astype(jnp.bfloat16))
    total, aligned = lax.scan(one_subject, jnp.zeros((n_frames, n_verts), jnp.float32), data)
    return (aligned, total / data.shape[0])
```

```python
import functools
import math

import jax
import jax.numpy as jnp
from jax import lax
from jax.experimental import pallas as pl
from jax.experimental.pallas import tpu as pltpu
from jax.sharding import PartitionSpec as P

NS_STEPS = 4
LANES = 128
ROWS = 8
BF16 = jnp.bfloat16
F32 = jnp.float32


def dot(a, b):
    return lax.dot_general(a, b, (((1,), (0,)), ((), ())), preferred_element_type=F32)


def dot_t(a, b):
    return lax.dot_general(a, b, (((1,), (1,)), ((), ())), preferred_element_type=F32)


def split(x):
    hi = x.astype(BF16)
    return hi, (x - hi.astype(F32)).astype(BF16)


def halves(x):
    mid = x.shape[1] // 2
    return x[:, :mid] + x[:, mid:]


def polar_factor_t(z):
    norm_sq = jnp.sum(z * z, keepdims=True)
    z = z / jnp.sqrt(norm_sq + 1e-06)
    for _ in range(NS_STEPS):
        hi, lo = split(z)
        both = jnp.concatenate([hi, lo], axis=1)
        pair = jnp.concatenate(
            [jnp.concatenate([hi, hi], axis=1), jnp.concatenate([lo, lo], axis=1)], axis=0
        )
        gram = halves(dot_t(both, pair))
        g_hi, g_lo = split(gram)
        moved = halves(
            dot(jnp.concatenate([g_hi, g_lo], axis=1), jnp.concatenate([both, both], axis=0))
        )
        z = 1.5 * z - 0.5 * moved
    return z


def align_kernel(
    n_subjects, n_centres, group, pos_ref, nb_ref, data_ref, tmpl_ref, low_ref, high_ref,
    aligned_ref, partial_ref, low_out, high_out, edge_out, hits_out, wide, acc, hits, sems,
):
    k = nb_ref.shape[1]
    span = 2 * k
    own = data_ref.shape[2]
    frames = data_ref.shape[1]
    n_wide = own + 2 * k

    copies = []
    for i in range(n_subjects + 1):
        body = data_ref.at[i] if i < n_subjects else tmpl_ref
        copies.append(pltpu.make_async_copy(body, wide.at[i, :, pl.ds(k, own)], sems.at[i, 0]))
        copies.append(pltpu.make_async_copy(low_ref.at[i], wide.at[i, :, pl.ds(0, k)], sems.at[i, 1]))
        copies.append(
            pltpu.make_async_copy(high_ref.at[i], wide.at[i, :, pl.ds(k + own, k)], sems.at[i, 2])
        )
    for copy in copies:
        copy.start()
    acc[...] = jnp.zeros_like(acc)
    hits[...] = jnp.zeros_like(hits)
    for copy in copies:
        copy.wait()

    spot = lax.broadcasted_iota(jnp.int32, (span, k), 0)
    lane = lax.broadcasted_iota(jnp.int32, (1, k), 1)
    ones = jnp.ones((ROWS, k), BF16)

    def place(ref, first, keep, value):
        left, right = value[:, :k], value[:, k:]
        ref[:, pl.ds(first, k)] += jnp.where(keep, left, 0.0)
        ref[:, pl.ds(first + k, k)] += right
        ref[:, pl.ds(first + span, k)] += jnp.where(keep, 0.0, left)

    def one_group(step, carry):
        results = []
        for member in range(group):
            c = step * group + member
            pos = pos_ref[c]
            first = pl.multiple_of((pos // k) * k, k)
            off = pos - first
            keep = lane >= off
            want = (nb_ref[pl.ds(c, 1), :] + (k + off)) & (span - 1)
            pick = jnp.where(spot == want, 1.0, 0.0).astype(BF16)

            def window(i, first=first, keep=keep):
                a = wide[i, :, pl.ds(first, k)]
                b = wide[i, :, pl.ds(first + k, k)]
                d = wide[i, :, pl.ds(first + span, k)]
                return jnp.concatenate([jnp.where(keep, a, d), b], axis=1)

            xs = [dot(window(i), pick).astype(BF16) for i in range(n_subjects)]
            m_t = dot(window(n_subjects), pick).T.astype(BF16)
            crosses = dot(m_t, jnp.concatenate(xs, axis=1))
            outs = []
            for i in range(n_subjects):
                z = polar_factor_t(crosses[:, i * k : (i + 1) * k])
                hi, lo = split(z)
                spread = dot(pick, jnp.concatenate([hi, lo], axis=1)).astype(BF16)
                outs.append(dot_t(jnp.concatenate([xs[i], xs[i]], axis=1), spread))
            results.append((first, keep, outs, dot_t(ones, pick)))
        for first, keep, outs, count in results:
            for i in range(n_subjects):
                place(acc.at[i], first, keep, outs[i])
            place(hits, first, keep, count)
        return carry

    lax.fori_loop(0, n_centres // group, one_group, 0)

    low_out[:, :frames, :] = acc[:, :, :k]
    high_out[:, :frames, :] = acc[:, :, own + k :]
    for i in range(n_subjects):
        low_out[i, frames:, :] = hits[:, :k]
        high_out[i, frames:, :] = hits[:, own + k :]
    edge_out[:, :, :k] = acc[:, :, k:span]
    edge_out[:, :, k:] = acc[:, :, own : own + k]
    hits_out[:, :k] = hits[:, k:span]
    hits_out[:, k:] = hits[:, own : own + k]
    inverse = 1.0 / jnp.maximum(hits[:, k : k + own], 1.0)

    def one_rows(step, carry):
        rows = pl.ds(pl.multiple_of(step * 2 * ROWS, 2 * ROWS), 2 * ROWS)
        scale = jnp.concatenate([inverse, inverse], axis=0)
        total = jnp.zeros((2 * ROWS, own), F32)
        for i in range(n_subjects):
            mapped = acc[i, rows, k : k + own] * scale
            aligned_ref[i, rows, :] = mapped.astype(BF16)
            total = total + mapped
        partial_ref[rows, :] = total
        return carry

    lax.fori_loop(0, frames // (2 * ROWS), one_rows, 0)


def align(data, template, low, high, local_pos, neighbours):
    n_subjects, frames, own = data.shape
    n_centres, k = neighbours.shape
    n_wide = own + 2 * k
    group = 2 if n_centres % 2 == 0 else 1
    vmem = pl.BlockSpec(memory_space=pltpu.VMEM)
    hbm = pl.BlockSpec(memory_space=pl.ANY)
    smem = pl.BlockSpec(memory_space=pltpu.SMEM)
    return pl.pallas_call(
        functools.partial(align_kernel, n_subjects, n_centres, group),
        out_shape=(
            jax.ShapeDtypeStruct((n_subjects, frames, own), BF16),
            jax.ShapeDtypeStruct((frames, own), F32),
            jax.ShapeDtypeStruct((n_subjects, frames + ROWS, k), F32),
            jax.ShapeDtypeStruct((n_subjects, frames + ROWS, k), F32),
            jax.ShapeDtypeStruct((n_subjects, frames, 2 * k), F32),
            jax.ShapeDtypeStruct((ROWS, 2 * k), F32),
        ),
        in_specs=[smem, vmem, hbm, hbm, hbm, hbm],
        out_specs=(vmem,) * 6,
        scratch_shapes=[
            pltpu.VMEM((n_subjects + 1, frames, n_wide), BF16),
            pltpu.VMEM((n_subjects, frames, n_wide), F32),
            pltpu.VMEM((ROWS, n_wide), F32),
            pltpu.SemaphoreType.DMA((n_subjects + 1, 3)),
        ],
        compiler_params=pltpu.CompilerParams(vmem_limit_bytes=48 * 1024 * 1024),
        name="align",
    )(local_pos, neighbours, data, template, low, high)


def along_vert(up_value, down_value):
    size = lax.axis_size("vert")
    up = [(i, i + 1) for i in range(size - 1)]
    down = [(i + 1, i) for i in range(size - 1)]
    return lax.ppermute(up_value, "vert", up), lax.ppermute(down_value, "vert", down)


class Hypercube:
    def __init__(self):
        self.size = lax.axis_size("subj")
        self.verts = lax.axis_size("vert")
        n_bits = self.size.bit_length() - 1
        bits = list(range(n_bits))
        self.phases = [bits[i : i + 2] for i in range(0, n_bits, 2)]

    def order(self, phase, v):
        return phase if v % 2 == 0 else phase[::-1]

    def mine(self, phase):
        s = lax.axis_index("subj")

        def number(bits):
            return sum(((s >> b) & 1) << i for i, b in enumerate(bits))

        even = number(self.order(phase, 0))
        odd = number(self.order(phase, 1))
        return jnp.where(lax.axis_index("vert") % 2 == 0, even, odd)

    def pairs(self, phase, m):
        out = []
        for s in range(self.size):
            for v in range(self.verts):
                mask = sum(((m >> i) & 1) << b for i, b in enumerate(self.order(phase, v)))
                out.append((s * self.verts + v, (s ^ mask) * self.verts + v))
        return out

    def swap(self, value, phase, m):
        return lax.ppermute(value, ("subj", "vert"), self.pairs(phase, m))

    def reduce(self, total, top):
        for phase in self.phases:
            count = 1 << len(phase)
            rows = total.shape[0] // count
            j = self.mine(phase)
            inverse = 1024.0 / top[0, 0]
            got = []
            for m in range(1, count):
                block = lax.dynamic_slice_in_dim(total, (j ^ m) * rows, rows)
                sent = (block * inverse).astype(jnp.float16)
                got.append((self.swap(sent, phase, m), self.swap(top, phase, m)))
            total = lax.dynamic_slice_in_dim(total, j * rows, rows)
            for value, other in got:
                total = total + value.astype(F32) * (other[0, 0] * (1.0 / 1024.0))
                top = jnp.maximum(top, other)
        return total, top

    def gather(self, value):
        for phase in reversed(self.phases):
            count = 1 << len(phase)
            j = self.mine(phase)
            parts = [value] + [self.swap(value, phase, m) for m in range(1, count)]
            placed = []
            for q in range(count):
                chosen = parts[0]
                for m in range(1, count):
                    chosen = jnp.where((j ^ q) == m, parts[m], chosen)
                placed.append(chosen)
            value = jnp.concatenate(placed, axis=0)
        return value


def local(data, template, centres, neighbours):
    k = neighbours.shape[1]
    n_subjects, frames, own = data.shape
    everything_low = jnp.concatenate([data[:, :, :k], template[None, :, :k]], axis=0)
    everything_high = jnp.concatenate([data[:, :, own - k :], template[None, :, own - k :]], axis=0)
    low, high = along_vert(everything_high, everything_low)
    local_pos = centres - lax.axis_index("vert") * own
    aligned, partial, low_out, high_out, edges, edge_hits = align(
        data, template, low, high, local_pos, neighbours
    )
    from_low, from_high = along_vert(high_out, low_out)
    total_edges = edges + jnp.concatenate([from_low[:, :frames], from_high[:, :frames]], axis=2)
    more_hits = jnp.concatenate([from_low[0, frames], from_high[0, frames]], axis=0)
    mapped = total_edges / jnp.maximum(edge_hits[0] + more_hits, 1.0)
    rounded = mapped.astype(BF16)
    aligned = aligned.at[:, :, :k].set(rounded[:, :, :k])
    aligned = aligned.at[:, :, own - k :].set(rounded[:, :, k:])
    edge_sum = jnp.sum(mapped, axis=0)
    partial = partial.at[:, :k].set(edge_sum[:, :k])
    partial = partial.at[:, own - k :].set(edge_sum[:, k:])
    top = jnp.maximum(jnp.max(jnp.abs(partial)), 1e-30)
    cube = Hypercube()
    total, top = cube.reduce(partial, jnp.full((ROWS, LANES), top, F32))
    subjects = n_subjects * lax.axis_size("subj")
    sent = (total * (1024.0 / top[0, 0])).astype(jnp.float16)
    whole = cube.gather(sent)
    return aligned, whole.astype(F32) * (top[0, 0] * (1.0 / (1024.0 * subjects)))


def solution(mesh):
    in_specs = (P("subj", None, "vert"), P(None, "vert"), P("vert"), P("vert", None))
    out_specs = (P("subj", None, "vert"), P(None, "vert"))
    return jax.shard_map(local, mesh=mesh, in_specs=in_specs, out_specs=out_specs, check_vma=False)
```

```python
import functools
import math

import jax
import jax.numpy as jnp
from jax import lax
from jax.experimental import pallas as pl
from jax.experimental.pallas import tpu as pltpu
from jax.sharding import PartitionSpec as P

NS_STEPS = 4
LANES = 128
ROWS = 8
HEADROOM = 10.0
BF16 = jnp.bfloat16
F32 = jnp.float32


def dot(a, b):
    return lax.dot_general(a, b, (((1,), (0,)), ((), ())), preferred_element_type=F32)


def dot_t(a, b):
    return lax.dot_general(a, b, (((1,), (1,)), ((), ())), preferred_element_type=F32)


def split(x):
    hi = x.astype(BF16)
    return hi, (x - hi.astype(F32)).astype(BF16)


def halves(x):
    mid = x.shape[1] // 2
    return x[:, :mid] + x[:, mid:]


def polar_factors_t(zs):
    sums = [jnp.sum(z * z, keepdims=True) for z in zs]
    zs = [z / jnp.sqrt(norm_sq + 1e-06) for z, norm_sq in zip(zs, sums)]
    for _ in range(NS_STEPS):
        boths = [jnp.concatenate(split(z), axis=1) for z in zs]
        grams = []
        for both in boths:
            k = both.shape[0]
            hi, lo = both[:, :k], both[:, k:]
            pair = jnp.concatenate(
                [jnp.concatenate([hi, hi], axis=1), jnp.concatenate([lo, lo], axis=1)], axis=0
            )
            grams.append(dot_t(both, pair))
        grams = [jnp.concatenate(split(halves(gram)), axis=1) for gram in grams]
        moved = [
            dot(gram, jnp.concatenate([both, both], axis=0)) for gram, both in zip(grams, boths)
        ]
        zs = [1.5 * z - 0.5 * halves(move) for z, move in zip(zs, moved)]
    return zs


def align_kernel(
    n_subjects, n_centres, group, side_ref, pos_ref, nb_ref, data_ref, tmpl_ref, low_ref, high_ref,
    aligned_ref, first_ref, rest_ref, low_out, high_out, edge_out, hits_out, wide, acc, hits, sems,
):
    k = nb_ref.shape[1]
    span = 2 * k
    own = data_ref.shape[2]
    frames = data_ref.shape[1]

    copies = []
    for i in range(n_subjects + 1):
        body = data_ref.at[i] if i < n_subjects else tmpl_ref
        copies.append(pltpu.make_async_copy(body, wide.at[i, :, pl.ds(k, own)], sems.at[i, 0]))
        copies.append(pltpu.make_async_copy(low_ref.at[i], wide.at[i, :, pl.ds(0, k)], sems.at[i, 1]))
        copies.append(
            pltpu.make_async_copy(high_ref.at[i], wide.at[i, :, pl.ds(k + own, k)], sems.at[i, 2])
        )
    for copy in copies:
        copy.start()
    acc[...] = jnp.zeros_like(acc)
    hits[...] = jnp.zeros_like(hits)
    for copy in copies:
        copy.wait()

    @pl.when(side_ref[0] == 0)
    def _():
        wide[:, :, :k] = jnp.zeros((n_subjects + 1, frames, k), BF16)

    @pl.when(side_ref[1] == 0)
    def _():
        wide[:, :, k + own :] = jnp.zeros((n_subjects + 1, frames, k), BF16)

    spot = lax.broadcasted_iota(jnp.int32, (span, k), 0)
    lane = lax.broadcasted_iota(jnp.int32, (1, k), 1)
    ones = jnp.ones((ROWS, k), BF16)

    def place(ref, first, keep, value):
        left, right = value[:, :k], value[:, k:]
        ref[:, pl.ds(first, k)] += jnp.where(keep, left, 0.0)
        ref[:, pl.ds(first + k, k)] += right
        ref[:, pl.ds(first + span, k)] += jnp.where(keep, 0.0, left)

    def one_group(step, carry):
        members = []
        for member in range(group):
            c = step * group + member
            pos = pos_ref[c]
            first = pl.multiple_of((pos // k) * k, k)
            off = pos - first
            keep = lane >= off
            want = (nb_ref[pl.ds(c, 1), :] + (k + off)) & (span - 1)
            pick = jnp.where(spot == want, 1.0, 0.0).astype(BF16)
            members.append((first, keep, pick))

        def window(i, first, keep):
            a = wide[i, :, pl.ds(first, k)]
            b = wide[i, :, pl.ds(first + k, k)]
            d = wide[i, :, pl.ds(first + span, k)]
            return jnp.concatenate([jnp.where(keep, a, d), b], axis=1)

        xs = []
        m_ts = []
        for first, keep, pick in members:
            for i in range(n_subjects):
                xs.append(dot(window(i, first, keep), pick).astype(BF16))
            m_ts.append(dot(window(n_subjects, first, keep), pick))
        m_ts = [m.T.astype(BF16) for m in m_ts]
        zs = []
        for member in range(group):
            mine = xs[member * n_subjects : (member + 1) * n_subjects]
            crosses = dot(m_ts[member], jnp.concatenate(mine, axis=1))
            zs += [crosses[:, i * k : (i + 1) * k] for i in range(n_subjects)]
        zs = polar_factors_t(zs)
        spreads = []
        for n, z in enumerate(zs):
            pick = members[n // n_subjects][2]
            spreads.append(dot(pick, jnp.concatenate(split(z), axis=1)).astype(BF16))
        outs = [
            dot_t(jnp.concatenate([x, x], axis=1), spread) for x, spread in zip(xs, spreads)
        ]
        for member, (first, keep, pick) in enumerate(members):
            for i in range(n_subjects):
                place(acc.at[i], first, keep, outs[member * n_subjects + i])
            place(hits, first, keep, dot_t(ones, pick))
        return carry

    lax.fori_loop(0, n_centres // group, one_group, 0)

    low_out[:, :frames, :] = acc[:, :, :k]
    high_out[:, :frames, :] = acc[:, :, own + k :]
    for i in range(n_subjects):
        low_out[i, frames:, :] = hits[:, :k]
        high_out[i, frames:, :] = hits[:, own + k :]
    edge_out[:, :, :k] = acc[:, :, k:span]
    edge_out[:, :, k:] = acc[:, :, own : own + k]
    hits_out[:, :k] = hits[:, k:span]
    hits_out[:, k:] = hits[:, own : own + k]
    half = own // 2
    hits[...] = 1.0 / jnp.maximum(hits[...], 1.0)
    scale = hits[:, span:own]

    def one_rows(step, top):
        rows = pl.ds(pl.multiple_of(step * 2 * ROWS, 2 * ROWS), 2 * ROWS)
        both = jnp.concatenate([scale, scale], axis=0)
        total = jnp.zeros((2 * ROWS, own - span), F32)
        for i in range(n_subjects):
            mapped = acc[i, rows, span:own] * both
            aligned_ref[i, rows, k : own - k] = mapped.astype(BF16)
            total = total + mapped
        first_ref[rows, :half] = total[:, :half]
        rest_ref[rows, :] = total[:, half:]
        tops = jnp.abs(total[:, :half])
        while tops.shape[1] > k:
            tops = jnp.maximum(tops[:, : tops.shape[1] // 2], tops[:, tops.shape[1] // 2 :])
        return jnp.maximum(top, tops)

    top = lax.fori_loop(0, frames // (2 * ROWS), one_rows, jnp.zeros((2 * ROWS, k), F32))
    scale_out(first_ref, jnp.max(top, keepdims=True))


def scale_out(ref, top):
    width = ref.shape[1] - LANES
    power = jnp.clip(jnp.ceil(jnp.log(jnp.maximum(top, 1e-30)) * (1.0 / math.log(2.0))), -99.0, 99.0)
    ref[:, :width] = ref[:, :width] * jnp.exp2(HEADROOM - power)
    ref[:, width:] = jnp.broadcast_to(power, (ref.shape[0], LANES))


def align(data, template, low, high, sides, local_pos, neighbours):
    n_subjects, frames, own = data.shape
    n_centres, k = neighbours.shape
    n_wide = own + 2 * k
    group = math.gcd(n_centres, 8)
    vmem = pl.BlockSpec(memory_space=pltpu.VMEM)
    hbm = pl.BlockSpec(memory_space=pl.ANY)
    smem = pl.BlockSpec(memory_space=pltpu.SMEM)
    return pl.pallas_call(
        functools.partial(align_kernel, n_subjects, n_centres, group),
        out_shape=(
            jax.ShapeDtypeStruct((n_subjects, frames, own), BF16),
            jax.ShapeDtypeStruct((frames, own // 2 + LANES), F32),
            jax.ShapeDtypeStruct((frames, own // 2 - 2 * k), F32),
            jax.ShapeDtypeStruct((n_subjects, frames + ROWS, k), F32),
            jax.ShapeDtypeStruct((n_subjects, frames + ROWS, k), F32),
            jax.ShapeDtypeStruct((n_subjects, frames, 2 * k), F32),
            jax.ShapeDtypeStruct((ROWS, 2 * k), F32),
        ),
        in_specs=[smem, smem, vmem, hbm, hbm, hbm, hbm],
        out_specs=(vmem,) * 7,
        scratch_shapes=[
            pltpu.VMEM((n_subjects + 1, frames, n_wide), BF16),
            pltpu.VMEM((n_subjects, frames, n_wide), F32),
            pltpu.VMEM((ROWS, n_wide), F32),
            pltpu.SemaphoreType.DMA((n_subjects + 1, 3)),
        ],
        compiler_params=pltpu.CompilerParams(vmem_limit_bytes=32 * 1024 * 1024),
        name="align",
    )(sides, local_pos, neighbours, data, template, low, high)


def edges_kernel(
    n_subjects, side_ref, edge_ref, hits_ref, low_ref, high_ref, rest_ref, before_ref,
    aligned_ref, out_ref, left, right, sems,
):
    k = low_ref.shape[2]
    frames = edge_ref.shape[1]
    own = aligned_ref.shape[2]
    inner = rest_ref.shape[1]
    out_ref[:, :inner] = rest_ref[...]
    copies = []
    for n, (got_ref, block) in enumerate(((low_ref, left), (high_ref, right))):
        lanes = slice(n * k, (n + 1) * k)
        there = side_ref[n] > 0
        counts = hits_ref[:, lanes] + jnp.where(there, got_ref[0, frames:, :], 0.0)
        inverse = (1.0 / jnp.maximum(counts, 1.0))[:1]
        total = jnp.zeros((frames, k), F32)
        for i in range(n_subjects):
            mapped = edge_ref[i, :, lanes] + jnp.where(there, got_ref[i, :frames, :], 0.0)
            mapped = mapped * inverse
            block[i] = mapped.astype(BF16)
            total = total + mapped
        out_ref[:, inner + n * k : inner + (n + 1) * k] = total
        copy = pltpu.make_async_copy(
            block, aligned_ref.at[:, :, pl.ds(n * (own - k), k)], sems.at[n]
        )
        copy.start()
        copies.append(copy)
    scale_out(out_ref, jnp.max(jnp.abs(out_ref[:, : inner + 2 * k]), keepdims=True))
    for copy in copies:
        copy.wait()


def finish_edges(edges, edge_hits, from_low, from_high, sides, rest, aligned):
    n_subjects, frames, _ = edges.shape
    k = from_low.shape[2]
    vmem = pl.BlockSpec(memory_space=pltpu.VMEM)
    hbm = pl.BlockSpec(memory_space=pl.ANY)
    smem = pl.BlockSpec(memory_space=pltpu.SMEM)
    return pl.pallas_call(
        functools.partial(edges_kernel, n_subjects),
        out_shape=(
            jax.ShapeDtypeStruct(aligned.shape, BF16),
            jax.ShapeDtypeStruct((frames, rest.shape[1] + 2 * k + LANES), F32),
        ),
        in_specs=[smem, vmem, vmem, vmem, vmem, vmem, hbm],
        out_specs=(hbm, vmem),
        input_output_aliases={6: 0},
        scratch_shapes=[
            pltpu.VMEM((n_subjects, frames, k), BF16),
            pltpu.VMEM((n_subjects, frames, k), BF16),
            pltpu.SemaphoreType.DMA((2,)),
        ],
        compiler_params=pltpu.CompilerParams(vmem_limit_bytes=16 * 1024 * 1024),
        name="edges",
    )(sides, edges, edge_hits, from_low, from_high, rest, aligned)


def along_vert(up_value, down_value):
    size = lax.axis_size("vert")
    if size == 2:
        sent = jnp.where(lax.axis_index("vert") == 0, up_value, down_value)
        got = lax.ppermute(sent, "vert", [(0, 1), (1, 0)])
        return got, got
    up = [(i, i + 1) for i in range(size - 1)]
    down = [(i + 1, i) for i in range(size - 1)]
    return lax.ppermute(up_value, "vert", up), lax.ppermute(down_value, "vert", down)


class Hypercube:
    def __init__(self):
        self.size = lax.axis_size("subj")
        self.verts = lax.axis_size("vert")
        n_bits = self.size.bit_length() - 1
        bits = list(range(n_bits))
        self.phases = [bits[i : i + 2] for i in range(0, n_bits, 2)]

    def order(self, phase, v):
        return phase if v % 2 == 0 else phase[::-1]

    def mine(self, phase):
        s = lax.axis_index("subj")

        def number(bits):
            return sum(((s >> b) & 1) << i for i, b in enumerate(bits))

        even = number(self.order(phase, 0))
        odd = number(self.order(phase, 1))
        return jnp.where(lax.axis_index("vert") % 2 == 0, even, odd)

    def pairs(self, phase, m):
        out = []
        for s in range(self.size):
            for v in range(self.verts):
                mask = sum(((m >> i) & 1) << b for i, b in enumerate(self.order(phase, v)))
                out.append((s * self.verts + v, (s ^ mask) * self.verts + v))
        return out

    def swap(self, value, phase, m):
        return lax.ppermute(value, ("subj", "vert"), self.pairs(phase, m))

    def reduce(self, block):
        width = block.shape[1] - LANES
        for phase in self.phases:
            count = 1 << len(phase)
            rows = block.shape[0] // count
            j = self.mine(phase)
            parts = [lax.dynamic_slice_in_dim(block, j * rows, rows)]
            for m in range(1, count):
                sent = lax.dynamic_slice_in_dim(block, (j ^ m) * rows, rows).astype(jnp.float16)
                parts.append(self.swap(sent, phase, m).astype(F32))
            powers = [part[:, width : width + 1] for part in parts]
            top = functools.reduce(jnp.maximum, powers)
            total = sum(part[:, :width] * jnp.exp2(p - top) for part, p in zip(parts, powers))
            block = jnp.concatenate([total, jnp.broadcast_to(top, (rows, LANES))], axis=1)
        return block[:, :width], block[0, width]

    def gather(self, value):
        for phase in reversed(self.phases):
            count = 1 << len(phase)
            j = self.mine(phase)
            parts = [value] + [self.swap(value, phase, m) for m in range(1, count)]
            placed = []
            for q in range(count):
                chosen = parts[0]
                for m in range(1, count):
                    chosen = jnp.where((j ^ q) == m, parts[m], chosen)
                placed.append(chosen)
            value = jnp.concatenate(placed, axis=0)
        return value


def local(data, template, centres, neighbours):
    k = neighbours.shape[1]
    n_subjects, frames, own = data.shape
    v = lax.axis_index("vert")
    sides = jnp.stack([v > 0, v < lax.axis_size("vert") - 1]).astype(jnp.int32)
    first_edge = jnp.concatenate([data[:, :, :k], template[None, :, :k]], axis=0)
    last_edge = jnp.concatenate([data[:, :, own - k :], template[None, :, own - k :]], axis=0)
    low, high = along_vert(last_edge, first_edge)
    local_pos = centres - v * own
    aligned, first, rest, low_out, high_out, edges, edge_hits = align(
        data, template, low, high, sides, local_pos, neighbours
    )
    from_low, from_high = along_vert(high_out, low_out)
    aligned, rest = finish_edges(edges, edge_hits, from_low, from_high, sides, rest, aligned)
    cube = Hypercube()
    subjects = n_subjects * lax.axis_size("subj")
    wholes = []
    for block in (first, rest):
        total, power = cube.reduce(block)
        whole = cube.gather(total.astype(jnp.float16))
        wholes.append(whole.astype(F32) * (jnp.exp2(power - HEADROOM) * (1.0 / subjects)))
    begin, end = wholes
    inner = end.shape[1] - 2 * k
    new_template = jnp.concatenate(
        [end[:, inner : inner + k], begin, end[:, :inner], end[:, inner + k :]], axis=1
    )
    return aligned, new_template


def solution(mesh):
    in_specs = (P("subj", None, "vert"), P(None, "vert"), P("vert"), P("vert", None))
    out_specs = (P("subj", None, "vert"), P(None, "vert"))
    return jax.shard_map(local, mesh=mesh, in_specs=in_specs, out_specs=out_specs, check_vma=False)
```

```python
import functools
import math

import jax
import jax.numpy as jnp
from jax import lax
from jax.experimental import pallas as pl
from jax.experimental.pallas import tpu as pltpu
from jax.sharding import PartitionSpec as P

NS_STEPS = 4
LANES = 128
ROWS = 8
HEADROOM = 10.0
BF16 = jnp.bfloat16
F32 = jnp.float32


def dot(a, b):
    return lax.dot_general(a, b, (((1,), (0,)), ((), ())), preferred_element_type=F32)


def dot_t(a, b):
    return lax.dot_general(a, b, (((1,), (1,)), ((), ())), preferred_element_type=F32)


def split(x):
    hi = x.astype(BF16)
    return hi, (x - hi.astype(F32)).astype(BF16)


def halves(x):
    mid = x.shape[1] // 2
    return x[:, :mid] + x[:, mid:]


def polar_factors_t(zs):
    sums = [jnp.sum(z * z, keepdims=True) for z in zs]
    zs = [z / jnp.sqrt(norm_sq + 1e-06) for z, norm_sq in zip(zs, sums)]
    for _ in range(NS_STEPS):
        boths = [jnp.concatenate(split(z), axis=1) for z in zs]
        grams = []
        for both in boths:
            k = both.shape[0]
            hi, lo = both[:, :k], both[:, k:]
            pair = jnp.concatenate(
                [jnp.concatenate([hi, hi], axis=1), jnp.concatenate([lo, lo], axis=1)], axis=0
            )
            grams.append(dot_t(both, pair))
        grams = [jnp.concatenate(split(halves(gram)), axis=1) for gram in grams]
        moved = [
            dot(gram, jnp.concatenate([both, both], axis=0)) for gram, both in zip(grams, boths)
        ]
        zs = [1.5 * z - 0.5 * halves(move) for z, move in zip(zs, moved)]
    return zs


def align_kernel(
    n_subjects, n_centres, group, meta_ref, pos_ref, nb_ref, data_ref, tmpl_ref, low_ref, high_ref,
    aligned_ref, first_ref, rest_ref, low_out, high_out, low_edge, high_edge, hits_out,
    wide, acc, hits, sems,
):
    k = nb_ref.shape[1]
    span = 2 * k
    own = data_ref.shape[2]
    frames = data_ref.shape[1]

    copies = []
    for i in range(n_subjects + 1):
        body = data_ref.at[i] if i < n_subjects else tmpl_ref
        copies.append(pltpu.make_async_copy(body, wide.at[i, :, pl.ds(k, own)], sems.at[i, 0]))
        copies.append(pltpu.make_async_copy(low_ref.at[i], wide.at[i, :, pl.ds(0, k)], sems.at[i, 1]))
        copies.append(
            pltpu.make_async_copy(high_ref.at[i], wide.at[i, :, pl.ds(k + own, k)], sems.at[i, 2])
        )
    for copy in copies:
        copy.start()
    acc[...] = jnp.zeros_like(acc)
    hits[...] = jnp.zeros_like(hits)
    for copy in copies:
        copy.wait()

    @pl.when(meta_ref[0] == 0)
    def _():
        wide[:, :, :k] = jnp.zeros((n_subjects + 1, frames, k), BF16)

    @pl.when(meta_ref[1] == 0)
    def _():
        wide[:, :, k + own :] = jnp.zeros((n_subjects + 1, frames, k), BF16)

    spot = lax.broadcasted_iota(jnp.int32, (span, k), 0)
    lane = lax.broadcasted_iota(jnp.int32, (1, k), 1)
    ones = jnp.ones((ROWS, k), BF16)

    def place(ref, first, keep, value):
        left, right = value[:, :k], value[:, k:]
        ref[:, pl.ds(first, k)] += jnp.where(keep, left, 0.0)
        ref[:, pl.ds(first + k, k)] += right
        ref[:, pl.ds(first + span, k)] += jnp.where(keep, 0.0, left)

    def one_group(step, carry):
        members = []
        for member in range(group):
            c = step * group + member
            pos = pos_ref[c]
            first = pl.multiple_of((pos // k) * k, k)
            off = pos - first
            keep = lane >= off
            want = (nb_ref[pl.ds(c, 1), :] + off) & (span - 1)
            pick = jnp.where(spot == want, 1.0, 0.0).astype(BF16)
            members.append((first, keep, pick))

        def window(i, first, keep):
            a = wide[i, :, pl.ds(first, k)]
            b = wide[i, :, pl.ds(first + k, k)]
            d = wide[i, :, pl.ds(first + span, k)]
            return jnp.concatenate([jnp.where(keep, a, d), b], axis=1)

        xs = []
        m_ts = []
        for first, keep, pick in members:
            for i in range(n_subjects):
                xs.append(dot(window(i, first, keep), pick).astype(BF16))
            m_ts.append(dot(window(n_subjects, first, keep), pick))
        m_ts = [m.T.astype(BF16) for m in m_ts]
        zs = []
        for member in range(group):
            mine = xs[member * n_subjects : (member + 1) * n_subjects]
            crosses = dot(m_ts[member], jnp.concatenate(mine, axis=1))
            zs += [crosses[:, i * k : (i + 1) * k] for i in range(n_subjects)]
        zs = polar_factors_t(zs)
        spreads = []
        for n, z in enumerate(zs):
            pick = members[n // n_subjects][2]
            spreads.append(dot(pick, jnp.concatenate(split(z), axis=1)).astype(BF16))
        outs = [
            dot_t(jnp.concatenate([x, x], axis=1), spread) for x, spread in zip(xs, spreads)
        ]
        for member, (first, keep, pick) in enumerate(members):
            for i in range(n_subjects):
                place(acc.at[i], first, keep, outs[member * n_subjects + i])
            place(hits, first, keep, dot_t(ones, pick))
        return carry

    lax.fori_loop(0, n_centres // group, one_group, 0)

    low_out[:, :frames, :] = acc[:, :, :k]
    high_out[:, :frames, :] = acc[:, :, own + k :]
    for i in range(n_subjects):
        low_out[i, frames:, :] = hits[:, :k]
        high_out[i, frames:, :] = hits[:, own + k :]
    low_edge[...] = acc[:, :, k:span]
    high_edge[...] = acc[:, :, own : own + k]
    hits_out[:, :k] = hits[:, k:span]
    hits_out[:, k:] = hits[:, own : own + k]
    half = own // 2
    hits[...] = 1.0 / jnp.maximum(hits[...], 1.0)
    scale = hits[:, span:own]

    def one_rows(step, top):
        rows = pl.ds(pl.multiple_of(step * 2 * ROWS, 2 * ROWS), 2 * ROWS)
        both = jnp.concatenate([scale, scale], axis=0)
        total = jnp.zeros((2 * ROWS, own - span), F32)
        for i in range(n_subjects):
            mapped = acc[i, rows, span:own] * both
            aligned_ref[i, rows, k : own - k] = mapped.astype(BF16)
            total = total + mapped
        first_ref[rows, :half] = total[:, :half]
        rest_ref[rows, :] = total[:, half:]
        tops = jnp.abs(total[:, :half])
        while tops.shape[1] > k:
            tops = jnp.maximum(tops[:, : tops.shape[1] // 2], tops[:, tops.shape[1] // 2 :])
        return jnp.maximum(top, tops)

    top = lax.fori_loop(0, frames // (2 * ROWS), one_rows, jnp.zeros((2 * ROWS, k), F32))
    scale_out(first_ref, jnp.max(top, keepdims=True))


def scale_out(ref, top):
    width = ref.shape[1] - LANES
    power = jnp.clip(jnp.ceil(jnp.log(jnp.maximum(top, 1e-30)) * (1.0 / math.log(2.0))), -99.0, 99.0)
    ref[:, :width] = ref[:, :width] * jnp.exp2(HEADROOM - power)
    ref[:, width:] = jnp.broadcast_to(power, (ref.shape[0], LANES))


def align(data, template, low, high, meta, centres, neighbours):
    n_subjects, frames, own = data.shape
    n_centres, k = neighbours.shape
    n_wide = own + 2 * k
    group = math.gcd(n_centres, 8)
    vmem = pl.BlockSpec(memory_space=pltpu.VMEM)
    hbm = pl.BlockSpec(memory_space=pl.ANY)
    smem = pl.BlockSpec(memory_space=pltpu.SMEM)
    return pl.pallas_call(
        functools.partial(align_kernel, n_subjects, n_centres, group),
        out_shape=(
            jax.ShapeDtypeStruct((n_subjects, frames, own), BF16),
            jax.ShapeDtypeStruct((frames, own // 2 + LANES), F32),
            jax.ShapeDtypeStruct((frames, own // 2 - 2 * k), F32),
            jax.ShapeDtypeStruct((n_subjects, frames + ROWS, k), F32),
            jax.ShapeDtypeStruct((n_subjects, frames + ROWS, k), F32),
            jax.ShapeDtypeStruct((n_subjects, frames, k), F32),
            jax.ShapeDtypeStruct((n_subjects, frames, k), F32),
            jax.ShapeDtypeStruct((ROWS, 2 * k), F32),
        ),
        in_specs=[smem, smem, vmem, hbm, hbm, hbm, hbm],
        out_specs=(vmem,) * 8,
        scratch_shapes=[
            pltpu.VMEM((n_subjects + 1, frames, n_wide), BF16),
            pltpu.VMEM((n_subjects, frames, n_wide), F32),
            pltpu.VMEM((ROWS, n_wide), F32),
            pltpu.SemaphoreType.DMA((n_subjects + 1, 3)),
        ],
        compiler_params=pltpu.CompilerParams(vmem_limit_bytes=24 * 1024 * 1024),
        cost_estimate=pl.CostEstimate(flops=16_000_000_000, bytes_accessed=8_000_000, transcendentals=0),
        name="align",
    )(meta, centres, neighbours, data, template, low, high)


def edges_kernel(
    n_subjects, meta_ref, low_edge, high_edge, hits_ref, low_ref, high_ref, rest_ref, before_ref,
    aligned_ref, out_ref, left, right, sems,
):
    k = low_ref.shape[2]
    frames = low_edge.shape[1]
    own = aligned_ref.shape[2]
    inner = rest_ref.shape[1]
    out_ref[:, :inner] = rest_ref[...]
    copies = []
    ends = ((low_ref, low_edge, left), (high_ref, high_edge, right))
    for n, (got_ref, edge_ref, block) in enumerate(ends):
        lanes = slice(n * k, (n + 1) * k)
        there = meta_ref[n] > 0
        counts = hits_ref[:, lanes] + jnp.where(there, got_ref[0, frames:, :], 0.0)
        inverse = (1.0 / jnp.maximum(counts, 1.0))[:1]
        total = jnp.zeros((frames, k), F32)
        for i in range(n_subjects):
            mapped = edge_ref[i] + jnp.where(there, got_ref[i, :frames, :], 0.0)
            mapped = mapped * inverse
            block[i] = mapped.astype(BF16)
            total = total + mapped
        out_ref[:, inner + n * k : inner + (n + 1) * k] = total
        copy = pltpu.make_async_copy(
            block, aligned_ref.at[:, :, pl.ds(n * (own - k), k)], sems.at[n]
        )
        copy.start()
        copies.append(copy)
    scale_out(out_ref, jnp.max(jnp.abs(out_ref[:, : inner + 2 * k]), keepdims=True))
    for copy in copies:
        copy.wait()


def finish_edges(low_edge, high_edge, edge_hits, from_low, from_high, meta, rest, aligned):
    n_subjects, frames, _ = low_edge.shape
    k = from_low.shape[2]
    vmem = pl.BlockSpec(memory_space=pltpu.VMEM)
    hbm = pl.BlockSpec(memory_space=pl.ANY)
    smem = pl.BlockSpec(memory_space=pltpu.SMEM)
    return pl.pallas_call(
        functools.partial(edges_kernel, n_subjects),
        out_shape=(
            jax.ShapeDtypeStruct(aligned.shape, BF16),
            jax.ShapeDtypeStruct((frames, rest.shape[1] + 2 * k + LANES), F32),
        ),
        in_specs=[smem, vmem, vmem, vmem, vmem, vmem, vmem, hbm],
        out_specs=(hbm, vmem),
        input_output_aliases={7: 0},
        scratch_shapes=[
            pltpu.VMEM((n_subjects, frames, k), BF16),
            pltpu.VMEM((n_subjects, frames, k), BF16),
            pltpu.SemaphoreType.DMA((2,)),
        ],
        compiler_params=pltpu.CompilerParams(vmem_limit_bytes=8 * 1024 * 1024),
        cost_estimate=pl.CostEstimate(flops=1_000_000_000, bytes_accessed=2_000_000, transcendentals=0),
        name="edges",
    )(meta, low_edge, high_edge, edge_hits, from_low, from_high, rest, aligned)


def core_swap(value):
    return lax.ppermute(value, "vert", [(0, 1), (1, 0)])


def along_vert(up_value, down_value):
    size = lax.axis_size("vert")
    up = [(i, i + 1) for i in range(size - 1)]
    down = [(i + 1, i) for i in range(size - 1)]
    return lax.ppermute(up_value, "vert", up), lax.ppermute(down_value, "vert", down)


class Hypercube:
    def __init__(self):
        self.size = lax.axis_size("subj")
        self.verts = lax.axis_size("vert")
        n_bits = self.size.bit_length() - 1
        bits = list(range(n_bits))
        self.phases = [bits[i : i + 2] for i in range(0, n_bits, 2)]

    def order(self, phase, v):
        return phase if v % 2 == 0 else phase[::-1]

    def mine(self, phase):
        s = lax.axis_index("subj")

        def number(bits):
            return sum(((s >> b) & 1) << i for i, b in enumerate(bits))

        even = number(self.order(phase, 0))
        odd = number(self.order(phase, 1))
        return jnp.where(lax.axis_index("vert") % 2 == 0, even, odd)

    def pairs(self, phase, m):
        out = []
        for s in range(self.size):
            for v in range(self.verts):
                mask = sum(((m >> i) & 1) << b for i, b in enumerate(self.order(phase, v)))
                out.append((s * self.verts + v, (s ^ mask) * self.verts + v))
        return out

    def swap(self, value, phase, m):
        return lax.ppermute(value, ("subj", "vert"), self.pairs(phase, m))

    def reduce(self, block):
        width = block.shape[1] - LANES
        for phase in self.phases:
            count = 1 << len(phase)
            rows = block.shape[0] // count
            j = self.mine(phase)
            parts = [lax.dynamic_slice_in_dim(block, j * rows, rows)]
            for m in range(1, count):
                sent = lax.dynamic_slice_in_dim(block, (j ^ m) * rows, rows).astype(jnp.float16)
                parts.append(self.swap(sent, phase, m).astype(F32))
            powers = [part[:, width : width + 1] for part in parts]
            top = functools.reduce(jnp.maximum, powers)
            total = sum(part[:, :width] * jnp.exp2(p - top) for part, p in zip(parts, powers))
            block = jnp.concatenate([total, jnp.broadcast_to(top, (rows, LANES))], axis=1)
        return block[:, :width], block[:, width:]

    def gather(self, value):
        for phase in reversed(self.phases):
            count = 1 << len(phase)
            j = self.mine(phase)
            parts = [value] + [self.swap(value, phase, m) for m in range(1, count)]
            placed = []
            for q in range(count):
                chosen = parts[0]
                for m in range(1, count):
                    chosen = jnp.where((j ^ q) == m, parts[m], chosen)
                placed.append(chosen)
            value = jnp.concatenate(placed, axis=0)
        return value


def local(data, template, centres, neighbours):
    k = neighbours.shape[1]
    n_subjects, frames, own = data.shape
    v = lax.axis_index("vert")
    verts = lax.axis_size("vert")
    meta = jnp.stack([v > 0, v < verts - 1]).astype(jnp.int32)
    if verts == 2:
        start = jnp.where(v == 0, own - k, 0)
        facing = (
            lax.dynamic_slice_in_dim(data, start, k, 2),
            lax.dynamic_slice_in_dim(template, start, k, 1)[None],
        )
        low = high = core_swap(jnp.concatenate(facing, axis=0))
    else:
        first_edge = jnp.concatenate([data[:, :, :k], template[None, :, :k]], axis=0)
        last_edge = jnp.concatenate([data[:, :, own - k :], template[None, :, own - k :]], axis=0)
        low, high = along_vert(last_edge, first_edge)
    aligned, first, rest, low_out, high_out, low_edge, high_edge, edge_hits = align(
        data, template, low, high, meta, centres - v * own, neighbours + k
    )
    if verts == 2:
        from_low = from_high = core_swap(jnp.where(v == 0, high_out, low_out))
    else:
        from_low, from_high = along_vert(high_out, low_out)
    aligned, rest = finish_edges(
        low_edge, high_edge, edge_hits, from_low, from_high, meta, rest, aligned
    )
    first, rest = lax.optimization_barrier((first, rest))
    cube = Hypercube()
    subjects = n_subjects * lax.axis_size("subj")
    pieces = []
    for block in (first, rest):
        total, power = cube.reduce(block)
        rows = power.shape[0]
        whole = cube.gather(total.astype(jnp.float16)).astype(F32)
        scale = jnp.exp2(power[:, :1] - HEADROOM) * (1.0 / subjects)
        whole = whole.reshape(frames // rows, rows, -1) * scale[None]
        pieces.append(whole.reshape(frames, -1))
    begin, end = pieces
    inner = end.shape[1] - 2 * k
    new_template = jnp.concatenate(
        [end[:, inner : inner + k], begin, end[:, :inner], end[:, inner + k :]], axis=1
    )
    return aligned, new_template


def solution(mesh):
    in_specs = (P("subj", None, "vert"), P(None, "vert"), P("vert"), P("vert", None))
    out_specs = (P("subj", None, "vert"), P(None, "vert"))
    return jax.shard_map(local, mesh=mesh, in_specs=in_specs, out_specs=out_specs, check_vma=False)
```

```python
import functools
import math

import jax
import jax.numpy as jnp
from jax import lax
from jax.experimental import pallas as pl
from jax.experimental.pallas import tpu as pltpu
from jax.sharding import PartitionSpec as P

NS_STEPS = 4
LANES = 128
ROWS = 8
HEADROOM = 10.0
ORDER = {-2: (1,), 2: (1,), -4: (3, 2, 1), 4: (3, 2, 1)}
FIRST = 8
PARTS = 4
BF16 = jnp.bfloat16
F32 = jnp.float32


def dot(a, b):
    return lax.dot_general(a, b, (((1,), (0,)), ((), ())), preferred_element_type=F32)


def dot_t(a, b):
    return lax.dot_general(a, b, (((1,), (1,)), ((), ())), preferred_element_type=F32)


def split(x):
    hi = x.astype(BF16)
    return hi, (x - hi.astype(F32)).astype(BF16)


def halves(x):
    mid = x.shape[1] // 2
    return x[:, :mid] + x[:, mid:]


def polar_factors_t(zs):
    sums = [jnp.sum(z * z, keepdims=True) for z in zs]
    zs = [z / jnp.sqrt(norm_sq + 1e-06) for z, norm_sq in zip(zs, sums)]
    for _ in range(NS_STEPS):
        boths = [jnp.concatenate(split(z), axis=1) for z in zs]
        grams = []
        for both in boths:
            k = both.shape[0]
            hi, lo = both[:, :k], both[:, k:]
            pair = jnp.concatenate(
                [jnp.concatenate([hi, hi], axis=1), jnp.concatenate([lo, lo], axis=1)], axis=0
            )
            grams.append(dot_t(both, pair))
        grams = [jnp.concatenate(split(halves(gram)), axis=1) for gram in grams]
        moved = [
            dot(gram, jnp.concatenate([both, both], axis=0)) for gram, both in zip(grams, boths)
        ]
        zs = [1.5 * z - 0.5 * halves(move) for z, move in zip(zs, moved)]
    return zs


def align_kernel(
    n_subjects, n_centres, group, meta_ref, pos_ref, nb_ref, data_ref, tmpl_ref, low_ref, high_ref,
    aligned_ref, first_ref, rest_ref, low_out, high_out, low_edge, high_edge, hits_out,
    wide, acc, hits, rounded, sems, out_sems,
):
    k = nb_ref.shape[1]
    span = 2 * k
    own = data_ref.shape[2]
    frames = data_ref.shape[1]

    copies = []
    for i in range(n_subjects + 1):
        body = data_ref.at[i] if i < n_subjects else tmpl_ref
        copies.append(pltpu.make_async_copy(body, wide.at[i, :, pl.ds(k, own)], sems.at[i, 0]))
        copies.append(pltpu.make_async_copy(low_ref.at[i], wide.at[i, :, pl.ds(0, k)], sems.at[i, 1]))
        copies.append(
            pltpu.make_async_copy(high_ref.at[i], wide.at[i, :, pl.ds(k + own, k)], sems.at[i, 2])
        )
    for copy in copies:
        copy.start()
    acc[...] = jnp.zeros_like(acc)
    hits[...] = jnp.zeros_like(hits)
    for copy in copies:
        copy.wait()

    @pl.when(meta_ref[0] == 0)
    def _():
        wide[:, :, :k] = jnp.zeros((n_subjects + 1, frames, k), BF16)

    @pl.when(meta_ref[1] == 0)
    def _():
        wide[:, :, k + own :] = jnp.zeros((n_subjects + 1, frames, k), BF16)

    spot = lax.broadcasted_iota(jnp.int32, (span, k), 0)
    lane = lax.broadcasted_iota(jnp.int32, (1, k), 1)
    ones = jnp.ones((ROWS, k), BF16)

    def place(ref, first, keep, value):
        left, right = value[:, :k], value[:, k:]
        ref[:, pl.ds(first, k)] += jnp.where(keep, left, 0.0)
        ref[:, pl.ds(first + k, k)] += right
        ref[:, pl.ds(first + span, k)] += jnp.where(keep, 0.0, left)

    def one_group(step, carry):
        members = []
        for member in range(group):
            c = step * group + member
            pos = pos_ref[c]
            first = pl.multiple_of((pos // k) * k, k)
            off = pos - first
            keep = lane >= off
            want = (nb_ref[pl.ds(c, 1), :] + off) & (span - 1)
            pick = jnp.where(spot == want, 1.0, 0.0).astype(BF16)
            members.append((first, keep, pick))

        def window(i, first, keep):
            a = wide[i, :, pl.ds(first, k)]
            b = wide[i, :, pl.ds(first + k, k)]
            d = wide[i, :, pl.ds(first + span, k)]
            return jnp.concatenate([jnp.where(keep, a, d), b], axis=1)

        xs = []
        m_ts = []
        for first, keep, pick in members:
            for i in range(n_subjects):
                xs.append(dot(window(i, first, keep), pick).astype(BF16))
            m_ts.append(dot(window(n_subjects, first, keep), pick))
        m_ts = [m.T.astype(BF16) for m in m_ts]
        zs = []
        for member in range(group):
            mine = xs[member * n_subjects : (member + 1) * n_subjects]
            crosses = dot(m_ts[member], jnp.concatenate(mine, axis=1))
            zs += [crosses[:, i * k : (i + 1) * k] for i in range(n_subjects)]
        zs = polar_factors_t(zs)
        spreads = []
        for member, (_, _, pick) in enumerate(members):
            mine = [split(z) for z in zs[member * n_subjects : (member + 1) * n_subjects]]
            stacked = jnp.concatenate(
                [jnp.concatenate([part[n] for part in mine], axis=1) for n in (0, 1)], axis=0
            )
            spread = dot(jnp.concatenate([pick, pick], axis=1), stacked)
            for i in range(n_subjects):
                spreads.append(jnp.concatenate(split(spread[:, i * k : (i + 1) * k]), axis=1))
        outs = [
            dot_t(jnp.concatenate([x, x], axis=1), spread) for x, spread in zip(xs, spreads)
        ]
        for member, (first, keep, pick) in enumerate(members):
            for i in range(n_subjects):
                place(acc.at[i], first, keep, outs[member * n_subjects + i])
            place(hits, first, keep, dot_t(ones, pick))
        return carry

    lax.fori_loop(0, n_centres // group, one_group, 0)

    low_out[:, :frames, :] = acc[:, :, :k]
    high_out[:, :frames, :] = acc[:, :, own + k :]
    for i in range(n_subjects):
        low_out[i, frames:, :] = hits[:, :k]
        high_out[i, frames:, :] = hits[:, own + k :]
    low_edge[...] = acc[:, :, k:span]
    high_edge[...] = acc[:, :, own : own + k]
    hits_out[:, :k] = hits[:, k:span]
    hits_out[:, k:] = hits[:, own : own + k]
    half = first_ref.shape[1] - LANES
    hits[...] = 1.0 / jnp.maximum(hits[...], 1.0)
    scale = hits[:, span:own]

    def one_rows(step, top):
        rows = pl.ds(pl.multiple_of(step * 2 * ROWS, 2 * ROWS), 2 * ROWS)
        both = jnp.concatenate([scale, scale], axis=0)
        total = jnp.zeros((2 * ROWS, own - span), F32)
        for i in range(n_subjects):
            mapped = acc[i, rows, span:own] * both
            rounded[i, rows, :] = mapped.astype(BF16)
            total = total + mapped
        first_ref[rows, :half] = total[:, :half]
        rest_ref[rows, :] = total[:, half:]
        tops = jnp.abs(total[:, :half])
        for at in range(0, half, k):
            top = jnp.maximum(top, tops[:, at : at + k])
        return top

    top = jnp.zeros((2 * ROWS, k), F32)
    steps = frames // (2 * ROWS)
    copies = []
    for part in range(PARTS):
        top = lax.fori_loop(part * steps // PARTS, (part + 1) * steps // PARTS, one_rows, top)
        rows = pl.ds(part * frames // PARTS, frames // PARTS)
        copies.append(
            pltpu.make_async_copy(
                rounded.at[:, rows, :], aligned_ref.at[:, rows, pl.ds(k, own - span)], out_sems.at[part]
            )
        )
        copies[-1].start()
    scale_out(first_ref, jnp.max(top, keepdims=True))
    for copy in copies:
        copy.wait()


def scale_out(ref, top):
    width = ref.shape[1] - LANES
    power = jnp.clip(jnp.ceil(jnp.log(jnp.maximum(top, 1e-30)) * (1.0 / math.log(2.0))), -99.0, 99.0)
    ref[:, :width] = ref[:, :width] * jnp.exp2(HEADROOM - power)
    ref[:, width:] = jnp.broadcast_to(power, (ref.shape[0], LANES))


def align(data, template, low, high, meta, centres, neighbours):
    n_subjects, frames, own = data.shape
    n_centres, k = neighbours.shape
    n_wide = own + 2 * k
    group = math.gcd(n_centres, 8)
    begin = own // 16 * FIRST
    vmem = pl.BlockSpec(memory_space=pltpu.VMEM)
    hbm = pl.BlockSpec(memory_space=pl.ANY)
    smem = pl.BlockSpec(memory_space=pltpu.SMEM)
    return pl.pallas_call(
        functools.partial(align_kernel, n_subjects, n_centres, group),
        out_shape=(
            jax.ShapeDtypeStruct((n_subjects, frames, own), BF16),
            jax.ShapeDtypeStruct((frames, begin + LANES), F32),
            jax.ShapeDtypeStruct((frames, own - begin - 2 * k), F32),
            jax.ShapeDtypeStruct((n_subjects, frames + ROWS, k), F32),
            jax.ShapeDtypeStruct((n_subjects, frames + ROWS, k), F32),
            jax.ShapeDtypeStruct((n_subjects, frames, k), F32),
            jax.ShapeDtypeStruct((n_subjects, frames, k), F32),
            jax.ShapeDtypeStruct((ROWS, 2 * k), F32),
        ),
        in_specs=[smem, smem, vmem, hbm, hbm, hbm, hbm],
        out_specs=(hbm,) + (vmem,) * 7,
        scratch_shapes=[
            pltpu.VMEM((n_subjects + 1, frames, n_wide), BF16),
            pltpu.VMEM((n_subjects, frames, n_wide), F32),
            pltpu.VMEM((ROWS, n_wide), F32),
            pltpu.VMEM((n_subjects, frames, own - 2 * k), BF16),
            pltpu.SemaphoreType.DMA((n_subjects + 1, 3)),
            pltpu.SemaphoreType.DMA((PARTS,)),
        ],
        compiler_params=pltpu.CompilerParams(vmem_limit_bytes=24 * 1024 * 1024),
        cost_estimate=pl.CostEstimate(flops=16_000_000_000, bytes_accessed=8_000_000, transcendentals=0),
        name="align",
    )(meta, centres, neighbours, data, template, low, high)


def edges_kernel(
    n_subjects, meta_ref, low_edge, high_edge, hits_ref, low_ref, high_ref, rest_ref, before_ref,
    aligned_ref, out_ref, left, right, sems,
):
    k = low_ref.shape[2]
    frames = low_edge.shape[1]
    own = aligned_ref.shape[2]
    inner = rest_ref.shape[1]
    out_ref[:, :inner] = rest_ref[...]
    copies = []
    ends = ((low_ref, low_edge, left), (high_ref, high_edge, right))
    for n, (got_ref, edge_ref, block) in enumerate(ends):
        lanes = slice(n * k, (n + 1) * k)
        there = meta_ref[n] > 0
        counts = hits_ref[:, lanes] + jnp.where(there, got_ref[0, frames:, :], 0.0)
        inverse = (1.0 / jnp.maximum(counts, 1.0))[:1]
        total = jnp.zeros((frames, k), F32)
        for i in range(n_subjects):
            mapped = edge_ref[i] + jnp.where(there, got_ref[i, :frames, :], 0.0)
            mapped = mapped * inverse
            block[i] = mapped.astype(BF16)
            total = total + mapped
        out_ref[:, inner + n * k : inner + (n + 1) * k] = total
        copy = pltpu.make_async_copy(
            block, aligned_ref.at[:, :, pl.ds(n * (own - k), k)], sems.at[n]
        )
        copy.start()
        copies.append(copy)
    scale_out(out_ref, jnp.max(jnp.abs(out_ref[:, : inner + 2 * k]), keepdims=True))
    for copy in copies:
        copy.wait()


def finish_edges(low_edge, high_edge, edge_hits, from_low, from_high, meta, rest, aligned):
    n_subjects, frames, _ = low_edge.shape
    k = from_low.shape[2]
    vmem = pl.BlockSpec(memory_space=pltpu.VMEM)
    hbm = pl.BlockSpec(memory_space=pl.ANY)
    smem = pl.BlockSpec(memory_space=pltpu.SMEM)
    return pl.pallas_call(
        functools.partial(edges_kernel, n_subjects),
        out_shape=(
            jax.ShapeDtypeStruct(aligned.shape, BF16),
            jax.ShapeDtypeStruct((frames, rest.shape[1] + 2 * k + LANES), F32),
        ),
        in_specs=[smem, vmem, vmem, vmem, vmem, vmem, vmem, hbm],
        out_specs=(hbm, vmem),
        input_output_aliases={7: 0},
        scratch_shapes=[
            pltpu.VMEM((n_subjects, frames, k), BF16),
            pltpu.VMEM((n_subjects, frames, k), BF16),
            pltpu.SemaphoreType.DMA((2,)),
        ],
        compiler_params=pltpu.CompilerParams(vmem_limit_bytes=8 * 1024 * 1024),
        cost_estimate=pl.CostEstimate(flops=1_000_000_000, bytes_accessed=2_000_000, transcendentals=0),
        name="edges",
    )(meta, low_edge, high_edge, edge_hits, from_low, from_high, rest, aligned)


def core_swap(value):
    return lax.ppermute(value, "vert", [(0, 1), (1, 0)])


def along_vert(up_value, down_value):
    size = lax.axis_size("vert")
    up = [(i, i + 1) for i in range(size - 1)]
    down = [(i + 1, i) for i in range(size - 1)]
    return lax.ppermute(up_value, "vert", up), lax.ppermute(down_value, "vert", down)


class Hypercube:
    def __init__(self):
        self.size = lax.axis_size("subj")
        self.verts = lax.axis_size("vert")
        bits = list(range(self.size.bit_length() - 1))
        self.phases = [bits[i : i + 2] for i in range(0, len(bits), 2)]
        self.whole = []

    def order(self, phase, v):
        return phase if v % 2 == 0 else phase[::-1]

    def mine(self, phase):
        s = lax.axis_index("subj")

        def number(bits):
            return sum(((s >> b) & 1) << i for i, b in enumerate(bits))

        even = number(self.order(phase, 0))
        odd = number(self.order(phase, 1))
        return jnp.where(lax.axis_index("vert") % 2 == 0, even, odd)

    def pairs(self, phase, m):
        out = []
        for s in range(self.size):
            for v in range(self.verts):
                mask = sum(((m >> i) & 1) << b for i, b in enumerate(self.order(phase, v)))
                out.append((s * self.verts + v, (s ^ mask) * self.verts + v))
        return out

    def swap(self, value, phase, m):
        return lax.ppermute(value, ("subj", "vert"), self.pairs(phase, m))

    def combine(self, parts):
        width = parts[0].shape[1] - LANES
        powers = [part[:, width : width + 1] for part in parts]
        top = functools.reduce(jnp.maximum, powers)
        total = sum(part[:, :width] * jnp.exp2(p - top) for part, p in zip(parts, powers))
        return jnp.concatenate([total, jnp.broadcast_to(top, (total.shape[0], LANES))], axis=1)

    def reduce(self, block):
        for phase in self.phases:
            count = 1 << len(phase)
            rows = block.shape[0] // count
            j = self.mine(phase)
            parts = [lax.dynamic_slice_in_dim(block, j * rows, rows)]
            for m in ORDER[-count]:
                sent = lax.dynamic_slice_in_dim(block, (j ^ m) * rows, rows).astype(jnp.float16)
                parts.append(self.swap(sent, phase, m).astype(F32))
            block = self.combine(parts)
        for bit in self.whole:
            sent = block.astype(jnp.float16)
            got = self.swap(sent, [bit], 1)
            block = self.combine([sent.astype(F32), got.astype(F32)])
        width = block.shape[1] - LANES
        return block[:, :width], block[:, width:]

    def gather(self, value):
        for phase in reversed(self.phases):
            count = 1 << len(phase)
            j = self.mine(phase)
            got = {m: self.swap(value, phase, m) for m in ORDER[count]}
            parts = [value] + [got[m] for m in range(1, count)]
            placed = []
            for q in range(count):
                chosen = parts[0]
                for m in range(1, count):
                    chosen = jnp.where((j ^ q) == m, parts[m], chosen)
                placed.append(chosen)
            value = jnp.concatenate(placed, axis=0)
        return value


def local(data, template, centres, neighbours):
    k = neighbours.shape[1]
    n_subjects, frames, own = data.shape
    v = lax.axis_index("vert")
    verts = lax.axis_size("vert")
    meta = jnp.stack([v > 0, v < verts - 1]).astype(jnp.int32)
    if verts == 2:
        start = jnp.where(v == 0, own - k, 0)
        facing = (
            lax.dynamic_slice_in_dim(data, start, k, 2),
            lax.dynamic_slice_in_dim(template, start, k, 1)[None],
        )
        low = high = core_swap(jnp.concatenate(facing, axis=0))
    else:
        first_edge = jnp.concatenate([data[:, :, :k], template[None, :, :k]], axis=0)
        last_edge = jnp.concatenate([data[:, :, own - k :], template[None, :, own - k :]], axis=0)
        low, high = along_vert(last_edge, first_edge)
    aligned, first, rest, low_out, high_out, low_edge, high_edge, edge_hits = align(
        pltpu.with_memory_space_constraint(data, pltpu.HBM), pltpu.with_memory_space_constraint(template, pltpu.HBM), low, high, meta, centres - v * own, neighbours + k
    )
    if verts == 2:
        from_low = from_high = core_swap(jnp.where(v == 0, high_out, low_out))
    else:
        from_low, from_high = along_vert(high_out, low_out)
    aligned, rest = finish_edges(
        low_edge, high_edge, edge_hits, from_low, from_high, meta, rest, aligned
    )
    first, rest = lax.optimization_barrier((first, rest))
    cube = Hypercube()
    subjects = n_subjects * lax.axis_size("subj")
    pieces = []
    for block in (first, rest):
        total, power = cube.reduce(block)
        rows = power.shape[0]
        whole = cube.gather(total.astype(jnp.float16)).astype(F32)
        scale = jnp.exp2(power[:, :1] - HEADROOM) * (1.0 / subjects)
        whole = whole.reshape(frames // rows, rows, -1) * scale[None]
        pieces.append(whole.reshape(frames, -1))
    begin, end = pieces
    inner = end.shape[1] - 2 * k
    new_template = jnp.concatenate(
        [end[:, inner : inner + k], begin, end[:, :inner], end[:, inner + k :]], axis=1
    )
    return aligned, new_template


def solution(mesh):
    in_specs = (P("subj", None, "vert"), P(None, "vert"), P("vert"), P("vert", None))
    out_specs = (P("subj", None, "vert"), P(None, "vert"))
    return jax.shard_map(local, mesh=mesh, in_specs=in_specs, out_specs=out_specs, check_vma=False)
```

```python
import functools
import math

import jax
import jax.numpy as jnp
from jax import lax
from jax.experimental import pallas as pl
from jax.experimental.pallas import tpu as pltpu
from jax.sharding import PartitionSpec as P

NS_STEPS = 4
LANES = 128
ROWS = 8
HEADROOM = 10.0
ORDER = {-2: (1,), 2: (1,), -4: (3, 2, 1), 4: (3, 2, 1)}
FIRST = 8
PARTS = 4
BF16 = jnp.bfloat16
F32 = jnp.float32


def dot(a, b):
    return lax.dot_general(a, b, (((1,), (0,)), ((), ())), preferred_element_type=F32)


def dot_t(a, b):
    return lax.dot_general(a, b, (((1,), (1,)), ((), ())), preferred_element_type=F32)


def split(x):
    hi = x.astype(BF16)
    return hi, (x - hi.astype(F32)).astype(BF16)


def halves(x):
    mid = x.shape[1] // 2
    return x[:, :mid] + x[:, mid:]


def polar_factors_t(zs):
    sums = [jnp.sum(z * z, keepdims=True) for z in zs]
    zs = [z / jnp.sqrt(norm_sq + 1e-06) for z, norm_sq in zip(zs, sums)]
    for _ in range(NS_STEPS):
        boths = [jnp.concatenate(split(z), axis=1) for z in zs]
        k = zs[0].shape[0]
        flips = [both.T for both in boths]
        boths_t = [jnp.concatenate([f[:k], f[k:]], axis=1) for f in flips]
        grams = [dot(both, jnp.concatenate([bt, bt], axis=0)) for both, bt in zip(boths, boths_t)]
        grams = [jnp.concatenate(split(halves(gram)), axis=1) for gram in grams]
        moved = [
            dot(gram, jnp.concatenate([both, both], axis=0)) for gram, both in zip(grams, boths)
        ]
        zs = [1.5 * z - 0.5 * halves(move) for z, move in zip(zs, moved)]
    return zs


def align_kernel(
    n_subjects, n_centres, group, meta_ref, pos_ref, nb_ref, data_ref, tmpl_ref, low_ref, high_ref,
    aligned_ref, first_ref, rest_ref, low_out, high_out, low_edge, high_edge, hits_out,
    wide, acc, hits, rounded, sems, out_sems,
):
    k = nb_ref.shape[1]
    span = 2 * k
    own = data_ref.shape[2]
    frames = data_ref.shape[1]

    copies = []
    for i in range(n_subjects + 1):
        body = data_ref.at[i] if i < n_subjects else tmpl_ref
        copies.append(pltpu.make_async_copy(body, wide.at[i, :, pl.ds(k, own)], sems.at[i, 0]))
        copies.append(pltpu.make_async_copy(low_ref.at[i], wide.at[i, :, pl.ds(0, k)], sems.at[i, 1]))
        copies.append(
            pltpu.make_async_copy(high_ref.at[i], wide.at[i, :, pl.ds(k + own, k)], sems.at[i, 2])
        )
    for copy in copies:
        copy.start()
    acc[...] = jnp.zeros_like(acc)
    hits[...] = jnp.zeros_like(hits)
    for copy in copies:
        copy.wait()

    @pl.when(meta_ref[0] == 0)
    def _():
        wide[:, :, :k] = jnp.zeros((n_subjects + 1, frames, k), BF16)

    @pl.when(meta_ref[1] == 0)
    def _():
        wide[:, :, k + own :] = jnp.zeros((n_subjects + 1, frames, k), BF16)

    spot = lax.broadcasted_iota(jnp.int32, (span, k), 0)
    lane = lax.broadcasted_iota(jnp.int32, (1, k), 1)
    ones = jnp.ones((ROWS, k), BF16)

    def place(ref, first, keep, value):
        left, right = value[:, :k], value[:, k:]
        ref[:, pl.ds(first, k)] += jnp.where(keep, left, 0.0)
        ref[:, pl.ds(first + k, k)] += right
        ref[:, pl.ds(first + span, k)] += jnp.where(keep, 0.0, left)

    def one_group(step, carry):
        members = []
        for member in range(group):
            c = step * group + member
            pos = pos_ref[c]
            first = pl.multiple_of((pos // k) * k, k)
            off = pos - first
            keep = lane >= off
            want = (nb_ref[pl.ds(c, 1), :] + off) & (span - 1)
            pick = jnp.where(spot == want, 1.0, 0.0).astype(BF16)
            members.append((first, keep, pick))

        def window(i, first, keep):
            a = wide[i, :, pl.ds(first, k)]
            b = wide[i, :, pl.ds(first + k, k)]
            d = wide[i, :, pl.ds(first + span, k)]
            return jnp.concatenate([jnp.where(keep, a, d), b], axis=1)

        xs = []
        m_ts = []
        for first, keep, pick in members:
            rows = [window(i, first, keep) for i in range(n_subjects + 1)]
            picked = dot(jnp.concatenate(rows, axis=0), pick).astype(BF16)
            frames = rows[0].shape[0]
            xs += [picked[i * frames : (i + 1) * frames] for i in range(n_subjects)]
            m_ts.append(picked[n_subjects * frames :])
        m_ts = [m.T for m in m_ts]
        zs = []
        for member in range(group):
            mine = xs[member * n_subjects : (member + 1) * n_subjects]
            crosses = dot(m_ts[member], jnp.concatenate(mine, axis=1))
            zs += [crosses[:, i * k : (i + 1) * k] for i in range(n_subjects)]
        zs = polar_factors_t(zs)
        spreads = []
        for member, (_, _, pick) in enumerate(members):
            mine = [split(z) for z in zs[member * n_subjects : (member + 1) * n_subjects]]
            stacked = jnp.concatenate(
                [jnp.concatenate([part[n] for part in mine], axis=1) for n in (0, 1)], axis=0
            )
            spread = dot(jnp.concatenate([pick, pick], axis=1), stacked)
            for i in range(n_subjects):
                spreads.append(jnp.concatenate(split(spread[:, i * k : (i + 1) * k]), axis=1))
        outs = [
            dot_t(jnp.concatenate([x, x], axis=1), spread) for x, spread in zip(xs, spreads)
        ]
        for member, (first, keep, pick) in enumerate(members):
            for i in range(n_subjects):
                place(acc.at[i], first, keep, outs[member * n_subjects + i])
            place(hits, first, keep, dot_t(ones, pick))
        return carry

    lax.fori_loop(0, n_centres // group, one_group, 0)

    low_out[:, :frames, :] = acc[:, :, :k]
    high_out[:, :frames, :] = acc[:, :, own + k :]
    for i in range(n_subjects):
        low_out[i, frames:, :] = hits[:, :k]
        high_out[i, frames:, :] = hits[:, own + k :]
    low_edge[...] = acc[:, :, k:span]
    high_edge[...] = acc[:, :, own : own + k]
    hits_out[:, :k] = hits[:, k:span]
    hits_out[:, k:] = hits[:, own : own + k]
    half = first_ref.shape[1] - LANES
    hits[...] = 1.0 / jnp.maximum(hits[...], 1.0)
    scale = hits[:, span:own]

    def one_rows(step, top):
        rows = pl.ds(pl.multiple_of(step * 2 * ROWS, 2 * ROWS), 2 * ROWS)
        both = jnp.concatenate([scale, scale], axis=0)
        total = jnp.zeros((2 * ROWS, own - span), F32)
        for i in range(n_subjects):
            mapped = acc[i, rows, span:own] * both
            rounded[i, rows, :] = mapped.astype(BF16)
            total = total + mapped
        first_ref[rows, :half] = total[:, :half]
        rest_ref[rows, :] = total[:, half:]
        tops = jnp.abs(total[:, :half])
        for at in range(0, half, k):
            top = jnp.maximum(top, tops[:, at : at + k])
        return top

    top = jnp.zeros((2 * ROWS, k), F32)
    steps = frames // (2 * ROWS)
    copies = []
    for part in range(PARTS):
        top = lax.fori_loop(part * steps // PARTS, (part + 1) * steps // PARTS, one_rows, top)
        rows = pl.ds(part * frames // PARTS, frames // PARTS)
        copies.append(
            pltpu.make_async_copy(
                rounded.at[:, rows, :], aligned_ref.at[:, rows, pl.ds(k, own - span)], out_sems.at[part]
            )
        )
        copies[-1].start()
    scale_out(first_ref, jnp.max(top, keepdims=True))
    for copy in copies:
        copy.wait()


def scale_out(ref, top):
    width = ref.shape[1] - LANES
    power = jnp.clip(jnp.ceil(jnp.log(jnp.maximum(top, 1e-30)) * (1.0 / math.log(2.0))), -99.0, 99.0)
    ref[:, :width] = ref[:, :width] * jnp.exp2(HEADROOM - power)
    ref[:, width:] = jnp.broadcast_to(power, (ref.shape[0], LANES))


def align(data, template, low, high, meta, centres, neighbours):
    n_subjects, frames, own = data.shape
    n_centres, k = neighbours.shape
    n_wide = own + 2 * k
    group = math.gcd(n_centres, 8)
    begin = own // 16 * FIRST
    vmem = pl.BlockSpec(memory_space=pltpu.VMEM)
    hbm = pl.BlockSpec(memory_space=pl.ANY)
    smem = pl.BlockSpec(memory_space=pltpu.SMEM)
    return pl.pallas_call(
        functools.partial(align_kernel, n_subjects, n_centres, group),
        out_shape=(
            jax.ShapeDtypeStruct((n_subjects, frames, own), BF16),
            jax.ShapeDtypeStruct((frames, begin + LANES), F32),
            jax.ShapeDtypeStruct((frames, own - begin - 2 * k), F32),
            jax.ShapeDtypeStruct((n_subjects, frames + ROWS, k), F32),
            jax.ShapeDtypeStruct((n_subjects, frames + ROWS, k), F32),
            jax.ShapeDtypeStruct((n_subjects, frames, k), F32),
            jax.ShapeDtypeStruct((n_subjects, frames, k), F32),
            jax.ShapeDtypeStruct((ROWS, 2 * k), F32),
        ),
        in_specs=[smem, smem, vmem, hbm, hbm, hbm, hbm],
        out_specs=(hbm,) + (vmem,) * 7,
        scratch_shapes=[
            pltpu.VMEM((n_subjects + 1, frames, n_wide), BF16),
            pltpu.VMEM((n_subjects, frames, n_wide), F32),
            pltpu.VMEM((ROWS, n_wide), F32),
            pltpu.VMEM((n_subjects, frames, own - 2 * k), BF16),
            pltpu.SemaphoreType.DMA((n_subjects + 1, 3)),
            pltpu.SemaphoreType.DMA((PARTS,)),
        ],
        compiler_params=pltpu.CompilerParams(vmem_limit_bytes=24 * 1024 * 1024),
        cost_estimate=pl.CostEstimate(flops=16_000_000_000, bytes_accessed=8_000_000, transcendentals=0),
        name="align",
    )(meta, centres, neighbours, data, template, low, high)


def edges_kernel(
    n_subjects, meta_ref, low_edge, high_edge, hits_ref, low_ref, high_ref, rest_ref, before_ref,
    aligned_ref, out_ref, left, right, sems,
):
    k = low_ref.shape[2]
    frames = low_edge.shape[1]
    own = aligned_ref.shape[2]
    inner = rest_ref.shape[1]
    out_ref[:, :inner] = rest_ref[...]
    copies = []
    ends = ((low_ref, low_edge, left), (high_ref, high_edge, right))
    for n, (got_ref, edge_ref, block) in enumerate(ends):
        lanes = slice(n * k, (n + 1) * k)
        there = meta_ref[n] > 0
        counts = hits_ref[:, lanes] + jnp.where(there, got_ref[0, frames:, :], 0.0)
        inverse = (1.0 / jnp.maximum(counts, 1.0))[:1]
        total = jnp.zeros((frames, k), F32)
        for i in range(n_subjects):
            mapped = edge_ref[i] + jnp.where(there, got_ref[i, :frames, :], 0.0)
            mapped = mapped * inverse
            block[i] = mapped.astype(BF16)
            total = total + mapped
        out_ref[:, inner + n * k : inner + (n + 1) * k] = total
        copy = pltpu.make_async_copy(
            block, aligned_ref.at[:, :, pl.ds(n * (own - k), k)], sems.at[n]
        )
        copy.start()
        copies.append(copy)
    scale_out(out_ref, jnp.max(jnp.abs(out_ref[:, : inner + 2 * k]), keepdims=True))
    for copy in copies:
        copy.wait()


def finish_edges(low_edge, high_edge, edge_hits, from_low, from_high, meta, rest, aligned):
    n_subjects, frames, _ = low_edge.shape
    k = from_low.shape[2]
    vmem = pl.BlockSpec(memory_space=pltpu.VMEM)
    hbm = pl.BlockSpec(memory_space=pl.ANY)
    smem = pl.BlockSpec(memory_space=pltpu.SMEM)
    return pl.pallas_call(
        functools.partial(edges_kernel, n_subjects),
        out_shape=(
            jax.ShapeDtypeStruct(aligned.shape, BF16),
            jax.ShapeDtypeStruct((frames, rest.shape[1] + 2 * k + LANES), F32),
        ),
        in_specs=[smem, vmem, vmem, vmem, vmem, vmem, vmem, hbm],
        out_specs=(hbm, vmem),
        input_output_aliases={7: 0},
        scratch_shapes=[
            pltpu.VMEM((n_subjects, frames, k), BF16),
            pltpu.VMEM((n_subjects, frames, k), BF16),
            pltpu.SemaphoreType.DMA((2,)),
        ],
        compiler_params=pltpu.CompilerParams(vmem_limit_bytes=8 * 1024 * 1024),
        cost_estimate=pl.CostEstimate(flops=1_000_000_000, bytes_accessed=2_000_000, transcendentals=0),
        name="edges",
    )(meta, low_edge, high_edge, edge_hits, from_low, from_high, rest, aligned)


def core_swap(value):
    return lax.ppermute(value, "vert", [(0, 1), (1, 0)])


def along_vert(up_value, down_value):
    size = lax.axis_size("vert")
    up = [(i, i + 1) for i in range(size - 1)]
    down = [(i + 1, i) for i in range(size - 1)]
    return lax.ppermute(up_value, "vert", up), lax.ppermute(down_value, "vert", down)


class Hypercube:
    def __init__(self):
        self.size = lax.axis_size("subj")
        self.verts = lax.axis_size("vert")
        bits = list(range(self.size.bit_length() - 1))
        self.phases = [bits[i : i + 2] for i in range(0, len(bits), 2)]
        self.whole = []

    def order(self, phase, v):
        return phase if v % 2 == 0 else phase[::-1]

    def mine(self, phase):
        s = lax.axis_index("subj")

        def number(bits):
            return sum(((s >> b) & 1) << i for i, b in enumerate(bits))

        even = number(self.order(phase, 0))
        odd = number(self.order(phase, 1))
        return jnp.where(lax.axis_index("vert") % 2 == 0, even, odd)

    def pairs(self, phase, m):
        out = []
        for s in range(self.size):
            for v in range(self.verts):
                mask = sum(((m >> i) & 1) << b for i, b in enumerate(self.order(phase, v)))
                out.append((s * self.verts + v, (s ^ mask) * self.verts + v))
        return out

    def swap(self, value, phase, m):
        return lax.ppermute(value, ("subj", "vert"), self.pairs(phase, m))

    def combine(self, parts):
        width = parts[0].shape[1] - LANES
        powers = [part[:, width : width + 1] for part in parts]
        top = functools.reduce(jnp.maximum, powers)
        total = sum(part[:, :width] * jnp.exp2(p - top) for part, p in zip(parts, powers))
        return jnp.concatenate([total, jnp.broadcast_to(top, (total.shape[0], LANES))], axis=1)

    def reduce(self, block):
        for phase in self.phases:
            count = 1 << len(phase)
            rows = block.shape[0] // count
            j = self.mine(phase)
            parts = [lax.dynamic_slice_in_dim(block, j * rows, rows)]
            for m in ORDER[-count]:
                sent = lax.dynamic_slice_in_dim(block, (j ^ m) * rows, rows).astype(jnp.float16)
                parts.append(self.swap(sent, phase, m).astype(F32))
            block = self.combine(parts)
        for bit in self.whole:
            sent = block.astype(jnp.float16)
            got = self.swap(sent, [bit], 1)
            block = self.combine([sent.astype(F32), got.astype(F32)])
        width = block.shape[1] - LANES
        return block[:, :width], block[:, width:]

    def gather(self, value):
        for phase in reversed(self.phases):
            count = 1 << len(phase)
            j = self.mine(phase)
            got = {m: self.swap(value, phase, m) for m in ORDER[count]}
            parts = [value] + [got[m] for m in range(1, count)]
            placed = []
            for q in range(count):
                chosen = parts[0]
                for m in range(1, count):
                    chosen = jnp.where((j ^ q) == m, parts[m], chosen)
                placed.append(chosen)
            value = jnp.concatenate(placed, axis=0)
        return value


def local(data, template, centres, neighbours):
    k = neighbours.shape[1]
    n_subjects, frames, own = data.shape
    v = lax.axis_index("vert")
    verts = lax.axis_size("vert")
    meta = jnp.stack([v > 0, v < verts - 1]).astype(jnp.int32)
    if verts == 2:
        start = jnp.where(v == 0, own - k, 0)
        facing = (
            lax.dynamic_slice_in_dim(data, start, k, 2),
            lax.dynamic_slice_in_dim(template, start, k, 1)[None],
        )
        low = high = core_swap(jnp.concatenate(facing, axis=0))
    else:
        first_edge = jnp.concatenate([data[:, :, :k], template[None, :, :k]], axis=0)
        last_edge = jnp.concatenate([data[:, :, own - k :], template[None, :, own - k :]], axis=0)
        low, high = along_vert(last_edge, first_edge)
    aligned, first, rest, low_out, high_out, low_edge, high_edge, edge_hits = align(
        pltpu.with_memory_space_constraint(data, pltpu.HBM), pltpu.with_memory_space_constraint(template, pltpu.HBM), low, high, meta, centres - v * own, neighbours + k
    )
    if verts == 2:
        from_low = from_high = core_swap(jnp.where(v == 0, high_out, low_out))
    else:
        from_low, from_high = along_vert(high_out, low_out)
    aligned, rest = finish_edges(
        low_edge, high_edge, edge_hits, from_low, from_high, meta, rest, aligned
    )
    first, rest = lax.optimization_barrier((first, rest))
    cube = Hypercube()
    subjects = n_subjects * lax.axis_size("subj")
    pieces = []
    for block in (first, rest):
        total, power = cube.reduce(block)
        rows = power.shape[0]
        whole = cube.gather(total.astype(jnp.float16)).astype(F32)
        scale = jnp.exp2(power[:, :1] - HEADROOM) * (1.0 / subjects)
        whole = whole.reshape(frames // rows, rows, -1) * scale[None]
        pieces.append(whole.reshape(frames, -1))
    begin, end = pieces
    inner = end.shape[1] - 2 * k
    new_template = jnp.concatenate(
        [end[:, inner : inner + k], begin, end[:, :inner], end[:, inner + k :]], axis=1
    )
    return aligned, new_template


def solution(mesh):
    in_specs = (P("subj", None, "vert"), P(None, "vert"), P("vert"), P("vert", None))
    out_specs = (P("subj", None, "vert"), P(None, "vert"))
    return jax.shard_map(local, mesh=mesh, in_specs=in_specs, out_specs=out_specs, check_vma=False)
```

```python
import functools
import math

import jax
import jax.numpy as jnp
from jax import lax
from jax.experimental import pallas as pl
from jax.experimental.pallas import tpu as pltpu
from jax.sharding import PartitionSpec as P

NS_STEPS = 4
LANES = 128
ROWS = 8
HEADROOM = 10.0
ORDER = {-2: (1,), 2: (1,), -4: (3, 2, 1), 4: (3, 2, 1)}
FIRST = 8
PARTS = 4
BF16 = jnp.bfloat16
F32 = jnp.float32


def dot(a, b):
    return lax.dot_general(a, b, (((1,), (0,)), ((), ())), preferred_element_type=F32)


def dot_t(a, b):
    return lax.dot_general(a, b, (((1,), (1,)), ((), ())), preferred_element_type=F32)


def split(x):
    hi = x.astype(BF16)
    return hi, (x - hi.astype(F32)).astype(BF16)


def halves(x):
    mid = x.shape[1] // 2
    return x[:, :mid] + x[:, mid:]


def polar_factors_t(zs):
    sums = [jnp.sum(z * z, keepdims=True) for z in zs]
    zs = [z / jnp.sqrt(norm_sq + 1e-06) for z, norm_sq in zip(zs, sums)]
    for _ in range(NS_STEPS):
        boths = [jnp.concatenate(split(z), axis=1) for z in zs]
        k = zs[0].shape[0]
        flips = [both.T for both in boths]
        boths_t = [jnp.concatenate([f[:k], f[k:]], axis=1) for f in flips]
        grams = [dot(both, jnp.concatenate([bt, bt], axis=0)) for both, bt in zip(boths, boths_t)]
        grams = [jnp.concatenate(split(halves(gram)), axis=1) for gram in grams]
        moved = [
            dot(gram, jnp.concatenate([both, both], axis=0)) for gram, both in zip(grams, boths)
        ]
        zs = [1.5 * z - 0.5 * halves(move) for z, move in zip(zs, moved)]
    return zs


def align_kernel(
    n_subjects, n_centres, group, meta_ref, pos_ref, nb_ref, data_ref, tmpl_ref, low_ref, high_ref,
    aligned_ref, first_ref, rest_ref, low_out, high_out, low_edge, high_edge, hits_out,
    wide, acc, hits, rounded, sems, out_sems,
):
    k = nb_ref.shape[1]
    span = 2 * k
    own = data_ref.shape[2]
    frames = data_ref.shape[1]

    copies = []
    for i in range(n_subjects + 1):
        body = data_ref.at[i] if i < n_subjects else tmpl_ref
        copies.append(pltpu.make_async_copy(body, wide.at[i, :, pl.ds(k, own)], sems.at[i, 0]))
        copies.append(pltpu.make_async_copy(low_ref.at[i], wide.at[i, :, pl.ds(0, k)], sems.at[i, 1]))
        copies.append(
            pltpu.make_async_copy(high_ref.at[i], wide.at[i, :, pl.ds(k + own, k)], sems.at[i, 2])
        )
    for copy in copies:
        copy.start()
    acc[...] = jnp.zeros_like(acc)
    hits[...] = jnp.zeros_like(hits)
    for copy in copies:
        copy.wait()

    @pl.when(meta_ref[0] == 0)
    def _():
        wide[:, :, :k] = jnp.zeros((n_subjects + 1, frames, k), BF16)

    @pl.when(meta_ref[1] == 0)
    def _():
        wide[:, :, k + own :] = jnp.zeros((n_subjects + 1, frames, k), BF16)

    spot = lax.broadcasted_iota(jnp.int32, (span, k), 0)
    lane = lax.broadcasted_iota(jnp.int32, (1, k), 1)
    ones = jnp.ones((ROWS, k), BF16)

    def place(ref, first, keep, value):
        left, right = value[:, :k], value[:, k:]
        ref[:, pl.ds(first, k)] += jnp.where(keep, left, 0.0)
        ref[:, pl.ds(first + k, k)] += right
        ref[:, pl.ds(first + span, k)] += jnp.where(keep, 0.0, left)

    def one_group(step, carry):
        members = []
        for member in range(group):
            c = step * group + member
            pos = pos_ref[c]
            first = pl.multiple_of((pos // k) * k, k)
            off = pos - first
            keep = lane >= off
            want = (nb_ref[pl.ds(c, 1), :] + off) & (span - 1)
            pick = jnp.where(spot == want, 1.0, 0.0).astype(BF16)
            members.append((first, keep, pick))

        def window(i, first, keep):
            a = wide[i, :, pl.ds(first, k)]
            b = wide[i, :, pl.ds(first + k, k)]
            d = wide[i, :, pl.ds(first + span, k)]
            return jnp.concatenate([jnp.where(keep, a, d), b], axis=1)

        xs = []
        m_ts = []
        for first, keep, pick in members:
            rows = [window(i, first, keep) for i in range(n_subjects + 1)]
            picked = dot(jnp.concatenate(rows, axis=0), pick).astype(BF16)
            frames = rows[0].shape[0]
            xs += [picked[i * frames : (i + 1) * frames] for i in range(n_subjects)]
            m_ts.append(picked[n_subjects * frames :])
        m_ts = [m.T for m in m_ts]
        zs = []
        for member in range(group):
            mine = xs[member * n_subjects : (member + 1) * n_subjects]
            crosses = dot(m_ts[member], jnp.concatenate(mine, axis=1))
            zs += [crosses[:, i * k : (i + 1) * k] for i in range(n_subjects)]
        zs = polar_factors_t(zs)
        spreads = []
        for member, (_, _, pick) in enumerate(members):
            mine = [split(z) for z in zs[member * n_subjects : (member + 1) * n_subjects]]
            stacked = jnp.concatenate(
                [jnp.concatenate([part[n] for part in mine], axis=1) for n in (0, 1)], axis=0
            )
            spread = dot(jnp.concatenate([pick, pick], axis=1), stacked)
            for i in range(n_subjects):
                spreads.append(jnp.concatenate(split(spread[:, i * k : (i + 1) * k]), axis=1))
        outs = [
            dot_t(jnp.concatenate([x, x], axis=1), spread) for x, spread in zip(xs, spreads)
        ]
        for member, (first, keep, pick) in enumerate(members):
            for i in range(n_subjects):
                place(acc.at[i], first, keep, outs[member * n_subjects + i])
            place(hits, first, keep, dot_t(ones, pick))
        return carry

    lax.fori_loop(0, n_centres // group, one_group, 0)

    low_out[:, :frames, :] = acc[:, :, :k]
    high_out[:, :frames, :] = acc[:, :, own + k :]
    for i in range(n_subjects):
        low_out[i, frames:, :] = hits[:, :k]
        high_out[i, frames:, :] = hits[:, own + k :]
    low_edge[...] = acc[:, :, k:span]
    high_edge[...] = acc[:, :, own : own + k]
    hits_out[:, :k] = hits[:, k:span]
    hits_out[:, k:] = hits[:, own : own + k]
    half = first_ref.shape[1] - LANES
    hits[...] = 1.0 / jnp.maximum(hits[...], 1.0)
    scale = hits[:, span:own]

    def one_rows(step, top):
        rows = pl.ds(pl.multiple_of(step * 2 * ROWS, 2 * ROWS), 2 * ROWS)
        both = jnp.concatenate([scale, scale], axis=0)
        total = jnp.zeros((2 * ROWS, own - span), F32)
        for i in range(n_subjects):
            mapped = acc[i, rows, span:own] * both
            rounded[i, rows, :] = mapped.astype(BF16)
            total = total + mapped
        first_ref[rows, :half] = total[:, :half]
        rest_ref[rows, :] = total[:, half:]
        tops = jnp.abs(total[:, :half])
        for at in range(0, half, k):
            top = jnp.maximum(top, tops[:, at : at + k])
        return top

    top = jnp.zeros((2 * ROWS, k), F32)
    steps = frames // (2 * ROWS)
    copies = []
    for part in range(PARTS):
        top = lax.fori_loop(part * steps // PARTS, (part + 1) * steps // PARTS, one_rows, top)
        rows = pl.ds(part * frames // PARTS, frames // PARTS)
        copies.append(
            pltpu.make_async_copy(
                rounded.at[:, rows, :], aligned_ref.at[:, rows, pl.ds(k, own - span)], out_sems.at[part]
            )
        )
        copies[-1].start()
    scale_out(first_ref, jnp.max(top, keepdims=True))
    for copy in copies:
        copy.wait()


def scale_out(ref, top):
    width = ref.shape[1] - LANES
    power = jnp.clip(jnp.ceil(jnp.log(jnp.maximum(top, 1e-30)) * (1.0 / math.log(2.0))), -99.0, 99.0)
    ref[:, :width] = ref[:, :width] * jnp.exp2(HEADROOM - power)
    ref[:, width:] = jnp.broadcast_to(power, (ref.shape[0], LANES))


def align(data, template, low, high, meta, centres, neighbours):
    n_subjects, frames, own = data.shape
    n_centres, k = neighbours.shape
    n_wide = own + 2 * k
    group = math.gcd(n_centres, 8)
    begin = own // 16 * FIRST
    vmem = pl.BlockSpec(memory_space=pltpu.VMEM)
    hbm = pl.BlockSpec(memory_space=pl.ANY)
    smem = pl.BlockSpec(memory_space=pltpu.SMEM)
    return pl.pallas_call(
        functools.partial(align_kernel, n_subjects, n_centres, group),
        out_shape=(
            jax.ShapeDtypeStruct((n_subjects, frames, own), BF16),
            jax.ShapeDtypeStruct((frames, begin + LANES), F32),
            jax.ShapeDtypeStruct((frames, own - begin - 2 * k), F32),
            jax.ShapeDtypeStruct((n_subjects, frames + ROWS, k), F32),
            jax.ShapeDtypeStruct((n_subjects, frames + ROWS, k), F32),
            jax.ShapeDtypeStruct((n_subjects, frames, k), F32),
            jax.ShapeDtypeStruct((n_subjects, frames, k), F32),
            jax.ShapeDtypeStruct((ROWS, 2 * k), F32),
        ),
        in_specs=[smem, smem, vmem, hbm, hbm, hbm, hbm],
        out_specs=(hbm,) + (vmem,) * 7,
        scratch_shapes=[
            pltpu.VMEM((n_subjects + 1, frames, n_wide), BF16),
            pltpu.VMEM((n_subjects, frames, n_wide), F32),
            pltpu.VMEM((ROWS, n_wide), F32),
            pltpu.VMEM((n_subjects, frames, own - 2 * k), BF16),
            pltpu.SemaphoreType.DMA((n_subjects + 1, 3)),
            pltpu.SemaphoreType.DMA((PARTS,)),
        ],
        compiler_params=pltpu.CompilerParams(vmem_limit_bytes=24 * 1024 * 1024),
        cost_estimate=pl.CostEstimate(flops=16_000_000_000, bytes_accessed=8_000_000, transcendentals=0),
        name="align",
    )(meta, centres, neighbours, data, template, low, high)


def edges_kernel(
    n_subjects, meta_ref, low_edge, high_edge, hits_ref, low_ref, high_ref, rest_ref, before_ref,
    aligned_ref, out_ref, left, right, sems,
):
    k = low_ref.shape[2]
    frames = low_edge.shape[1]
    own = aligned_ref.shape[2]
    inner = rest_ref.shape[1]
    out_ref[:, :inner] = rest_ref[...]
    copies = []
    ends = ((low_ref, low_edge, left), (high_ref, high_edge, right))
    for n, (got_ref, edge_ref, block) in enumerate(ends):
        lanes = slice(n * k, (n + 1) * k)
        there = meta_ref[n] > 0
        counts = hits_ref[:, lanes] + jnp.where(there, got_ref[0, frames:, :], 0.0)
        inverse = (1.0 / jnp.maximum(counts, 1.0))[:1]
        total = jnp.zeros((frames, k), F32)
        for i in range(n_subjects):
            mapped = edge_ref[i] + jnp.where(there, got_ref[i, :frames, :], 0.0)
            mapped = mapped * inverse
            block[i] = mapped.astype(BF16)
            total = total + mapped
        out_ref[:, inner + n * k : inner + (n + 1) * k] = total
        copy = pltpu.make_async_copy(
            block, aligned_ref.at[:, :, pl.ds(n * (own - k), k)], sems.at[n]
        )
        copy.start()
        copies.append(copy)
    scale_out(out_ref, jnp.max(jnp.abs(out_ref[:, : inner + 2 * k]), keepdims=True))
    for copy in copies:
        copy.wait()


def finish_edges(low_edge, high_edge, edge_hits, from_low, from_high, meta, rest, aligned):
    n_subjects, frames, _ = low_edge.shape
    k = from_low.shape[2]
    vmem = pl.BlockSpec(memory_space=pltpu.VMEM)
    hbm = pl.BlockSpec(memory_space=pl.ANY)
    smem = pl.BlockSpec(memory_space=pltpu.SMEM)
    return pl.pallas_call(
        functools.partial(edges_kernel, n_subjects),
        out_shape=(
            jax.ShapeDtypeStruct(aligned.shape, BF16),
            jax.ShapeDtypeStruct((frames, rest.shape[1] + 2 * k + LANES), F32),
        ),
        in_specs=[smem, vmem, vmem, vmem, vmem, vmem, vmem, hbm],
        out_specs=(hbm, vmem),
        input_output_aliases={7: 0},
        scratch_shapes=[
            pltpu.VMEM((n_subjects, frames, k), BF16),
            pltpu.VMEM((n_subjects, frames, k), BF16),
            pltpu.SemaphoreType.DMA((2,)),
        ],
        compiler_params=pltpu.CompilerParams(vmem_limit_bytes=8 * 1024 * 1024),
        cost_estimate=pl.CostEstimate(flops=1_000_000_000, bytes_accessed=2_000_000, transcendentals=0),
        name="edges",
    )(meta, low_edge, high_edge, edge_hits, from_low, from_high, rest, aligned)


def facing_kernel(start_ref, data_ref, tmpl_ref, out_ref, sems):
    n_subjects = data_ref.shape[0]
    k = out_ref.shape[2]
    lanes = pl.ds(pl.multiple_of(start_ref[0], k), k)
    copies = [pltpu.make_async_copy(tmpl_ref.at[:, lanes], out_ref.at[n_subjects], sems.at[n_subjects])]
    for i in range(n_subjects):
        copies.append(pltpu.make_async_copy(data_ref.at[i, :, lanes], out_ref.at[i], sems.at[i]))
    for copy in copies:
        copy.start()
    for copy in copies:
        copy.wait()


def facing_columns(data, template, start, k):
    n_subjects, frames, _ = data.shape
    vmem = pl.BlockSpec(memory_space=pltpu.VMEM)
    hbm = pl.BlockSpec(memory_space=pl.ANY)
    smem = pl.BlockSpec(memory_space=pltpu.SMEM)
    return pl.pallas_call(
        facing_kernel,
        out_shape=jax.ShapeDtypeStruct((n_subjects + 1, frames, k), BF16),
        in_specs=[smem, hbm, hbm],
        out_specs=vmem,
        scratch_shapes=[pltpu.SemaphoreType.DMA((n_subjects + 1,))],
        compiler_params=pltpu.CompilerParams(vmem_limit_bytes=4 * 1024 * 1024),
        cost_estimate=pl.CostEstimate(flops=0, bytes_accessed=800_000, transcendentals=0),
        name="facing",
    )(start, pltpu.with_memory_space_constraint(data, pltpu.HBM), pltpu.with_memory_space_constraint(template, pltpu.HBM))


def core_swap(value):
    return lax.ppermute(value, "vert", [(0, 1), (1, 0)])


def along_vert(up_value, down_value):
    size = lax.axis_size("vert")
    up = [(i, i + 1) for i in range(size - 1)]
    down = [(i + 1, i) for i in range(size - 1)]
    return lax.ppermute(up_value, "vert", up), lax.ppermute(down_value, "vert", down)


class Hypercube:
    def __init__(self):
        self.size = lax.axis_size("subj")
        self.verts = lax.axis_size("vert")
        bits = list(range(self.size.bit_length() - 1))
        self.phases = [bits[i : i + 2] for i in range(0, len(bits), 2)]
        self.whole = []

    def order(self, phase, v):
        return phase if v % 2 == 0 else phase[::-1]

    def mine(self, phase):
        s = lax.axis_index("subj")

        def number(bits):
            return sum(((s >> b) & 1) << i for i, b in enumerate(bits))

        even = number(self.order(phase, 0))
        odd = number(self.order(phase, 1))
        return jnp.where(lax.axis_index("vert") % 2 == 0, even, odd)

    def pairs(self, phase, m):
        out = []
        for s in range(self.size):
            for v in range(self.verts):
                mask = sum(((m >> i) & 1) << b for i, b in enumerate(self.order(phase, v)))
                out.append((s * self.verts + v, (s ^ mask) * self.verts + v))
        return out

    def swap(self, value, phase, m):
        return lax.ppermute(value, ("subj", "vert"), self.pairs(phase, m))

    def combine(self, parts):
        width = parts[0].shape[1] - LANES
        powers = [part[:, width : width + 1] for part in parts]
        top = functools.reduce(jnp.maximum, powers)
        total = sum(part[:, :width] * jnp.exp2(p - top) for part, p in zip(parts, powers))
        return jnp.concatenate([total, jnp.broadcast_to(top, (total.shape[0], LANES))], axis=1)

    def reduce(self, block):
        for phase in self.phases:
            count = 1 << len(phase)
            rows = block.shape[0] // count
            j = self.mine(phase)
            parts = [lax.dynamic_slice_in_dim(block, j * rows, rows)]
            for m in ORDER[-count]:
                sent = lax.dynamic_slice_in_dim(block, (j ^ m) * rows, rows).astype(jnp.float16)
                parts.append(self.swap(sent, phase, m).astype(F32))
            block = self.combine(parts)
        for bit in self.whole:
            sent = block.astype(jnp.float16)
            got = self.swap(sent, [bit], 1)
            block = self.combine([sent.astype(F32), got.astype(F32)])
        width = block.shape[1] - LANES
        return block[:, :width], block[:, width:]

    def gather(self, value):
        for phase in reversed(self.phases):
            count = 1 << len(phase)
            j = self.mine(phase)
            got = {m: self.swap(value, phase, m) for m in ORDER[count]}
            parts = [value] + [got[m] for m in range(1, count)]
            placed = []
            for q in range(count):
                chosen = parts[0]
                for m in range(1, count):
                    chosen = jnp.where((j ^ q) == m, parts[m], chosen)
                placed.append(chosen)
            value = jnp.concatenate(placed, axis=0)
        return value


def local(data, template, centres, neighbours):
    k = neighbours.shape[1]
    n_subjects, frames, own = data.shape
    v = lax.axis_index("vert")
    verts = lax.axis_size("vert")
    meta = jnp.stack([v > 0, v < verts - 1]).astype(jnp.int32)
    if verts == 2:
        start = jnp.where(v == 0, own - k, 0).astype(jnp.int32).reshape(1)
        low = high = core_swap(facing_columns(data, template, start, k))
    else:
        first_edge = jnp.concatenate([data[:, :, :k], template[None, :, :k]], axis=0)
        last_edge = jnp.concatenate([data[:, :, own - k :], template[None, :, own - k :]], axis=0)
        low, high = along_vert(last_edge, first_edge)
    aligned, first, rest, low_out, high_out, low_edge, high_edge, edge_hits = align(
        pltpu.with_memory_space_constraint(data, pltpu.HBM), pltpu.with_memory_space_constraint(template, pltpu.HBM), low, high, meta, centres - v * own, neighbours + k
    )
    if verts == 2:
        from_low = from_high = core_swap(jnp.where(v == 0, high_out, low_out))
    else:
        from_low, from_high = along_vert(high_out, low_out)
    aligned, rest = finish_edges(
        low_edge, high_edge, edge_hits, from_low, from_high, meta, rest, aligned
    )
    first, rest = lax.optimization_barrier((first, rest))
    cube = Hypercube()
    subjects = n_subjects * lax.axis_size("subj")
    pieces = []
    for block in (first, rest):
        total, power = cube.reduce(block)
        rows = power.shape[0]
        whole = cube.gather(total.astype(jnp.float16)).astype(F32)
        scale = jnp.exp2(power[:, :1] - HEADROOM) * (1.0 / subjects)
        whole = whole.reshape(frames // rows, rows, -1) * scale[None]
        pieces.append(whole.reshape(frames, -1))
    begin, end = pieces
    inner = end.shape[1] - 2 * k
    new_template = jnp.concatenate(
        [end[:, inner : inner + k], begin, end[:, :inner], end[:, inner + k :]], axis=1
    )
    return aligned, new_template


def solution(mesh):
    in_specs = (P("subj", None, "vert"), P(None, "vert"), P("vert"), P("vert", None))
    out_specs = (P("subj", None, "vert"), P(None, "vert"))
    return jax.shard_map(local, mesh=mesh, in_specs=in_specs, out_specs=out_specs, check_vma=False)
```

```python
import functools
import math

import jax
import jax.numpy as jnp
from jax import lax
from jax.experimental import pallas as pl
from jax.experimental.pallas import tpu as pltpu
from jax.sharding import PartitionSpec as P

NS_STEPS = 4
LANES = 128
ROWS = 8
HEADROOM = 10.0
ORDER = {-2: (1,), 2: (1,), -4: (3, 2, 1), 4: (3, 2, 1)}
FIRST = 8
PARTS = 4
BF16 = jnp.bfloat16
F32 = jnp.float32


def dot(a, b):
    return lax.dot_general(a, b, (((1,), (0,)), ((), ())), preferred_element_type=F32)


def dot_t(a, b):
    return lax.dot_general(a, b, (((1,), (1,)), ((), ())), preferred_element_type=F32)


def split(x):
    hi = x.astype(BF16)
    return hi, (x - hi.astype(F32)).astype(BF16)


def halves(x):
    mid = x.shape[1] // 2
    return x[:, :mid] + x[:, mid:]


def polar_factors_t(zs):
    sums = [jnp.sum(z * z, keepdims=True) for z in zs]
    zs = [z / jnp.sqrt(norm_sq + 1e-06) for z, norm_sq in zip(zs, sums)]
    for _ in range(NS_STEPS):
        boths = [jnp.concatenate(split(z), axis=1) for z in zs]
        k = zs[0].shape[0]
        flips = [both.T for both in boths]
        boths_t = [jnp.concatenate([f[:k], f[k:]], axis=1) for f in flips]
        grams = [dot(both, jnp.concatenate([bt, bt], axis=0)) for both, bt in zip(boths, boths_t)]
        grams = [jnp.concatenate(split(halves(gram)), axis=1) for gram in grams]
        moved = [
            dot(gram, jnp.concatenate([both, both], axis=0)) for gram, both in zip(grams, boths)
        ]
        zs = [1.5 * z - 0.5 * halves(move) for z, move in zip(zs, moved)]
    return zs


def align_kernel(
    n_subjects, n_centres, group, meta_ref, pos_ref, nb_ref, data_ref, tmpl_ref, low_ref, high_ref,
    aligned_ref, first_ref, rest_ref, low_out, high_out, low_edge, high_edge, hits_out,
    wide, acc, hits, rounded, sems, out_sems,
):
    k = nb_ref.shape[1]
    span = 2 * k
    own = data_ref.shape[2]
    frames = data_ref.shape[1]

    copies = []
    for i in range(n_subjects + 1):
        body = data_ref.at[i] if i < n_subjects else tmpl_ref
        copies.append(pltpu.make_async_copy(body, wide.at[i, :, pl.ds(k, own)], sems.at[i, 0]))
        copies.append(pltpu.make_async_copy(low_ref.at[i], wide.at[i, :, pl.ds(0, k)], sems.at[i, 1]))
        copies.append(
            pltpu.make_async_copy(high_ref.at[i], wide.at[i, :, pl.ds(k + own, k)], sems.at[i, 2])
        )
    for copy in copies:
        copy.start()
    acc[...] = jnp.zeros_like(acc)
    hits[...] = jnp.zeros_like(hits)
    for copy in copies:
        copy.wait()

    @pl.when(meta_ref[0] == 0)
    def _():
        wide[:, :, :k] = jnp.zeros((n_subjects + 1, frames, k), BF16)

    @pl.when(meta_ref[1] == 0)
    def _():
        wide[:, :, k + own :] = jnp.zeros((n_subjects + 1, frames, k), BF16)

    spot = lax.broadcasted_iota(jnp.int32, (span, k), 0)
    lane = lax.broadcasted_iota(jnp.int32, (1, k), 1)
    ones = jnp.ones((ROWS, k), BF16)

    def place(ref, first, keep, value):
        left, right = value[:, :k], value[:, k:]
        ref[:, pl.ds(first, k)] += jnp.where(keep, left, 0.0)
        ref[:, pl.ds(first + k, k)] += right
        ref[:, pl.ds(first + span, k)] += jnp.where(keep, 0.0, left)

    def one_group(step, carry):
        members = []
        for member in range(group):
            c = step * group + member
            pos = pos_ref[c]
            first = pl.multiple_of((pos // k) * k, k)
            off = pos - first
            keep = lane >= off
            want = (nb_ref[pl.ds(c, 1), :] + off) & (span - 1)
            pick = jnp.where(spot == want, 1.0, 0.0).astype(BF16)
            members.append((first, keep, pick))

        def window(i, first, keep):
            a = wide[i, :, pl.ds(first, k)]
            b = wide[i, :, pl.ds(first + k, k)]
            d = wide[i, :, pl.ds(first + span, k)]
            return jnp.concatenate([jnp.where(keep, a, d), b], axis=1)

        xs = []
        m_ts = []
        for first, keep, pick in members:
            rows = [window(i, first, keep) for i in range(n_subjects + 1)]
            picked = dot(jnp.concatenate(rows, axis=0), pick).astype(BF16)
            frames = rows[0].shape[0]
            xs += [picked[i * frames : (i + 1) * frames] for i in range(n_subjects)]
            m_ts.append(picked[n_subjects * frames :])
        m_ts = [m.T for m in m_ts]
        zs = []
        for member in range(group):
            mine = xs[member * n_subjects : (member + 1) * n_subjects]
            crosses = dot(m_ts[member], jnp.concatenate(mine, axis=1))
            zs += [crosses[:, i * k : (i + 1) * k] for i in range(n_subjects)]
        zs = polar_factors_t(zs)
        spreads = []
        for member, (_, _, pick) in enumerate(members):
            mine = [split(z) for z in zs[member * n_subjects : (member + 1) * n_subjects]]
            stacked = jnp.concatenate(
                [jnp.concatenate([part[n] for part in mine], axis=1) for n in (0, 1)], axis=0
            )
            spread = dot(jnp.concatenate([pick, pick], axis=1), stacked)
            for i in range(n_subjects):
                spreads.append(jnp.concatenate(split(spread[:, i * k : (i + 1) * k]), axis=1))
        outs = [
            dot_t(jnp.concatenate([x, x], axis=1), spread) for x, spread in zip(xs, spreads)
        ]
        for member, (first, keep, pick) in enumerate(members):
            for i in range(n_subjects):
                place(acc.at[i], first, keep, outs[member * n_subjects + i])
            place(hits, first, keep, dot_t(ones, pick))
        return carry

    lax.fori_loop(0, n_centres // group, one_group, 0)

    low_out[:, :frames, :] = acc[:, :, :k]
    high_out[:, :frames, :] = acc[:, :, own + k :]
    for i in range(n_subjects):
        low_out[i, frames:, :] = hits[:, :k]
        high_out[i, frames:, :] = hits[:, own + k :]
    low_edge[...] = acc[:, :, k:span]
    high_edge[...] = acc[:, :, own : own + k]
    hits_out[:, :k] = hits[:, k:span]
    hits_out[:, k:] = hits[:, own : own + k]
    half = first_ref.shape[1] - LANES
    hits[...] = 1.0 / jnp.maximum(hits[...], 1.0)
    scale = hits[:, span:own]

    def one_rows(step, top):
        rows = pl.ds(pl.multiple_of(step * 2 * ROWS, 2 * ROWS), 2 * ROWS)
        both = jnp.concatenate([scale, scale], axis=0)
        total = jnp.zeros((2 * ROWS, own - span), F32)
        for i in range(n_subjects):
            mapped = acc[i, rows, span:own] * both
            rounded[i, rows, :] = mapped.astype(BF16)
            total = total + mapped
        first_ref[rows, :half] = total[:, :half]
        rest_ref[rows, :] = total[:, half:]
        tops = jnp.abs(total[:, :half])
        for at in range(0, half, k):
            top = jnp.maximum(top, tops[:, at : at + k])
        return top

    top = jnp.zeros((2 * ROWS, k), F32)
    steps = frames // (2 * ROWS)
    copies = []
    for part in range(PARTS):
        top = lax.fori_loop(part * steps // PARTS, (part + 1) * steps // PARTS, one_rows, top)
        rows = pl.ds(part * frames // PARTS, frames // PARTS)
        copies.append(
            pltpu.make_async_copy(
                rounded.at[:, rows, :], aligned_ref.at[:, rows, pl.ds(k, own - span)], out_sems.at[part]
            )
        )
        copies[-1].start()
    scale_out(first_ref, jnp.max(top, keepdims=True))
    for copy in copies:
        copy.wait()


def scale_out(ref, top):
    width = ref.shape[1] - LANES
    power = jnp.clip(jnp.ceil(jnp.log(jnp.maximum(top, 1e-30)) * (1.0 / math.log(2.0))), -99.0, 99.0)
    ref[:, :width] = ref[:, :width] * jnp.exp2(HEADROOM - power)
    ref[:, width:] = jnp.broadcast_to(power, (ref.shape[0], LANES))


def align(data, template, low, high, meta, centres, neighbours):
    n_subjects, frames, own = data.shape
    n_centres, k = neighbours.shape
    n_wide = own + 2 * k
    group = math.gcd(n_centres, 16)
    begin = own // 16 * FIRST
    vmem = pl.BlockSpec(memory_space=pltpu.VMEM)
    hbm = pl.BlockSpec(memory_space=pl.ANY)
    smem = pl.BlockSpec(memory_space=pltpu.SMEM)
    return pl.pallas_call(
        functools.partial(align_kernel, n_subjects, n_centres, group),
        out_shape=(
            jax.ShapeDtypeStruct((n_subjects, frames, own), BF16),
            jax.ShapeDtypeStruct((frames, begin + LANES), F32),
            jax.ShapeDtypeStruct((frames, own - begin - 2 * k), F32),
            jax.ShapeDtypeStruct((n_subjects, frames + ROWS, k), F32),
            jax.ShapeDtypeStruct((n_subjects, frames + ROWS, k), F32),
            jax.ShapeDtypeStruct((n_subjects, frames, k), F32),
            jax.ShapeDtypeStruct((n_subjects, frames, k), F32),
            jax.ShapeDtypeStruct((ROWS, 2 * k), F32),
        ),
        in_specs=[smem, smem, vmem, hbm, hbm, hbm, hbm],
        out_specs=(hbm,) + (vmem,) * 7,
        scratch_shapes=[
            pltpu.VMEM((n_subjects + 1, frames, n_wide), BF16),
            pltpu.VMEM((n_subjects, frames, n_wide), F32),
            pltpu.VMEM((ROWS, n_wide), F32),
            pltpu.VMEM((n_subjects, frames, own - 2 * k), BF16),
            pltpu.SemaphoreType.DMA((n_subjects + 1, 3)),
            pltpu.SemaphoreType.DMA((PARTS,)),
        ],
        compiler_params=pltpu.CompilerParams(vmem_limit_bytes=24 * 1024 * 1024),
        cost_estimate=pl.CostEstimate(flops=16_000_000_000, bytes_accessed=8_000_000, transcendentals=0),
        name="align",
    )(meta, centres, neighbours, data, template, low, high)


def edges_kernel(
    n_subjects, meta_ref, low_edge, high_edge, hits_ref, low_ref, high_ref, rest_ref, before_ref,
    aligned_ref, out_ref, left, right, sems,
):
    k = low_ref.shape[2]
    frames = low_edge.shape[1]
    own = aligned_ref.shape[2]
    inner = rest_ref.shape[1]
    out_ref[:, :inner] = rest_ref[...]
    copies = []
    ends = ((low_ref, low_edge, left), (high_ref, high_edge, right))
    for n, (got_ref, edge_ref, block) in enumerate(ends):
        lanes = slice(n * k, (n + 1) * k)
        there = meta_ref[n] > 0
        counts = hits_ref[:, lanes] + jnp.where(there, got_ref[0, frames:, :], 0.0)
        inverse = (1.0 / jnp.maximum(counts, 1.0))[:1]
        total = jnp.zeros((frames, k), F32)
        for i in range(n_subjects):
            mapped = edge_ref[i] + jnp.where(there, got_ref[i, :frames, :], 0.0)
            mapped = mapped * inverse
            block[i] = mapped.astype(BF16)
            total = total + mapped
        out_ref[:, inner + n * k : inner + (n + 1) * k] = total
        copy = pltpu.make_async_copy(
            block, aligned_ref.at[:, :, pl.ds(n * (own - k), k)], sems.at[n]
        )
        copy.start()
        copies.append(copy)
    scale_out(out_ref, jnp.max(jnp.abs(out_ref[:, : inner + 2 * k]), keepdims=True))
    for copy in copies:
        copy.wait()


def finish_edges(low_edge, high_edge, edge_hits, from_low, from_high, meta, rest, aligned):
    n_subjects, frames, _ = low_edge.shape
    k = from_low.shape[2]
    vmem = pl.BlockSpec(memory_space=pltpu.VMEM)
    hbm = pl.BlockSpec(memory_space=pl.ANY)
    smem = pl.BlockSpec(memory_space=pltpu.SMEM)
    return pl.pallas_call(
        functools.partial(edges_kernel, n_subjects),
        out_shape=(
            jax.ShapeDtypeStruct(aligned.shape, BF16),
            jax.ShapeDtypeStruct((frames, rest.shape[1] + 2 * k + LANES), F32),
        ),
        in_specs=[smem, vmem, vmem, vmem, vmem, vmem, vmem, hbm],
        out_specs=(hbm, vmem),
        input_output_aliases={7: 0},
        scratch_shapes=[
            pltpu.VMEM((n_subjects, frames, k), BF16),
            pltpu.VMEM((n_subjects, frames, k), BF16),
            pltpu.SemaphoreType.DMA((2,)),
        ],
        compiler_params=pltpu.CompilerParams(vmem_limit_bytes=8 * 1024 * 1024),
        cost_estimate=pl.CostEstimate(flops=1_000_000_000, bytes_accessed=2_000_000, transcendentals=0),
        name="edges",
    )(meta, low_edge, high_edge, edge_hits, from_low, from_high, rest, aligned)


def facing_kernel(start_ref, data_ref, tmpl_ref, out_ref, sems):
    n_subjects = data_ref.shape[0]
    k = out_ref.shape[2]
    lanes = pl.ds(pl.multiple_of(start_ref[0], k), k)
    copies = [pltpu.make_async_copy(tmpl_ref.at[:, lanes], out_ref.at[n_subjects], sems.at[n_subjects])]
    for i in range(n_subjects):
        copies.append(pltpu.make_async_copy(data_ref.at[i, :, lanes], out_ref.at[i], sems.at[i]))
    for copy in copies:
        copy.start()
    for copy in copies:
        copy.wait()


def facing_columns(data, template, start, k):
    n_subjects, frames, _ = data.shape
    vmem = pl.BlockSpec(memory_space=pltpu.VMEM)
    hbm = pl.BlockSpec(memory_space=pl.ANY)
    smem = pl.BlockSpec(memory_space=pltpu.SMEM)
    return pl.pallas_call(
        facing_kernel,
        out_shape=jax.ShapeDtypeStruct((n_subjects + 1, frames, k), BF16),
        in_specs=[smem, hbm, hbm],
        out_specs=vmem,
        scratch_shapes=[pltpu.SemaphoreType.DMA((n_subjects + 1,))],
        compiler_params=pltpu.CompilerParams(vmem_limit_bytes=4 * 1024 * 1024),
        cost_estimate=pl.CostEstimate(flops=0, bytes_accessed=800_000, transcendentals=0),
        name="facing",
    )(start, pltpu.with_memory_space_constraint(data, pltpu.HBM), pltpu.with_memory_space_constraint(template, pltpu.HBM))


def core_swap(value):
    return lax.ppermute(value, "vert", [(0, 1), (1, 0)])


def along_vert(up_value, down_value):
    size = lax.axis_size("vert")
    up = [(i, i + 1) for i in range(size - 1)]
    down = [(i + 1, i) for i in range(size - 1)]
    return lax.ppermute(up_value, "vert", up), lax.ppermute(down_value, "vert", down)


class Hypercube:
    def __init__(self):
        self.size = lax.axis_size("subj")
        self.verts = lax.axis_size("vert")
        bits = list(range(self.size.bit_length() - 1))
        self.phases = [bits[i : i + 2] for i in range(0, len(bits), 2)]
        self.whole = []

    def order(self, phase, v):
        return phase if v % 2 == 0 else phase[::-1]

    def mine(self, phase):
        s = lax.axis_index("subj")

        def number(bits):
            return sum(((s >> b) & 1) << i for i, b in enumerate(bits))

        even = number(self.order(phase, 0))
        odd = number(self.order(phase, 1))
        return jnp.where(lax.axis_index("vert") % 2 == 0, even, odd)

    def pairs(self, phase, m):
        out = []
        for s in range(self.size):
            for v in range(self.verts):
                mask = sum(((m >> i) & 1) << b for i, b in enumerate(self.order(phase, v)))
                out.append((s * self.verts + v, (s ^ mask) * self.verts + v))
        return out

    def swap(self, value, phase, m):
        return lax.ppermute(value, ("subj", "vert"), self.pairs(phase, m))

    def combine(self, parts):
        width = parts[0].shape[1] - LANES
        powers = [part[:, width : width + 1] for part in parts]
        top = functools.reduce(jnp.maximum, powers)
        total = sum(part[:, :width] * jnp.exp2(p - top) for part, p in zip(parts, powers))
        return jnp.concatenate([total, jnp.broadcast_to(top, (total.shape[0], LANES))], axis=1)

    def reduce(self, block):
        for phase in self.phases:
            count = 1 << len(phase)
            rows = block.shape[0] // count
            j = self.mine(phase)
            parts = [lax.dynamic_slice_in_dim(block, j * rows, rows)]
            for m in ORDER[-count]:
                sent = lax.dynamic_slice_in_dim(block, (j ^ m) * rows, rows).astype(jnp.float16)
                parts.append(self.swap(sent, phase, m).astype(F32))
            block = self.combine(parts)
        for bit in self.whole:
            sent = block.astype(jnp.float16)
            got = self.swap(sent, [bit], 1)
            block = self.combine([sent.astype(F32), got.astype(F32)])
        width = block.shape[1] - LANES
        return block[:, :width], block[:, width:]

    def gather(self, value):
        for phase in reversed(self.phases):
            count = 1 << len(phase)
            j = self.mine(phase)
            got = {m: self.swap(value, phase, m) for m in ORDER[count]}
            parts = [value] + [got[m] for m in range(1, count)]
            placed = []
            for q in range(count):
                chosen = parts[0]
                for m in range(1, count):
                    chosen = jnp.where((j ^ q) == m, parts[m], chosen)
                placed.append(chosen)
            value = jnp.concatenate(placed, axis=0)
        return value


def local(data, template, centres, neighbours):
    k = neighbours.shape[1]
    n_subjects, frames, own = data.shape
    v = lax.axis_index("vert")
    verts = lax.axis_size("vert")
    meta = jnp.stack([v > 0, v < verts - 1]).astype(jnp.int32)
    if verts == 2:
        start = jnp.where(v == 0, own - k, 0).astype(jnp.int32).reshape(1)
        low = high = core_swap(facing_columns(data, template, start, k))
    else:
        first_edge = jnp.concatenate([data[:, :, :k], template[None, :, :k]], axis=0)
        last_edge = jnp.concatenate([data[:, :, own - k :], template[None, :, own - k :]], axis=0)
        low, high = along_vert(last_edge, first_edge)
    aligned, first, rest, low_out, high_out, low_edge, high_edge, edge_hits = align(
        pltpu.with_memory_space_constraint(data, pltpu.HBM), pltpu.with_memory_space_constraint(template, pltpu.HBM), low, high, meta, centres - v * own, neighbours + k
    )
    if verts == 2:
        from_low = from_high = core_swap(jnp.where(v == 0, high_out, low_out))
    else:
        from_low, from_high = along_vert(high_out, low_out)
    aligned, rest = finish_edges(
        low_edge, high_edge, edge_hits, from_low, from_high, meta, rest, aligned
    )
    first, rest = lax.optimization_barrier((first, rest))
    cube = Hypercube()
    subjects = n_subjects * lax.axis_size("subj")
    pieces = []
    for block in (first, rest):
        total, power = cube.reduce(block)
        rows = power.shape[0]
        whole = cube.gather(total.astype(jnp.float16)).astype(F32)
        scale = jnp.exp2(power[:, :1] - HEADROOM) * (1.0 / subjects)
        whole = whole.reshape(frames // rows, rows, -1) * scale[None]
        pieces.append(whole.reshape(frames, -1))
    begin, end = pieces
    inner = end.shape[1] - 2 * k
    new_template = jnp.concatenate(
        [end[:, inner : inner + k], begin, end[:, :inner], end[:, inner + k :]], axis=1
    )
    return aligned, new_template


def solution(mesh):
    in_specs = (P("subj", None, "vert"), P(None, "vert"), P("vert"), P("vert", None))
    out_specs = (P("subj", None, "vert"), P(None, "vert"))
    return jax.shard_map(local, mesh=mesh, in_specs=in_specs, out_specs=out_specs, check_vma=False)
```
